512 devices in a mesh: chan: 16 (over z_hi, y, core), lon: 32 (over x, z_lo).
Axes of the slice: x: 4, y: 4, z: 16 (z_hi: 2, z_lo: 8; z = z_hi * 8 + z_lo), core: 2. Of those that a mesh axis runs over, the one named last changes fastest.
Arguments:
- patches: bfloat16 [32, 128, 256, 128], P('chan', None, 'lon'), may hold values from -6 to 6
- embed_weight: bfloat16 [32, 128, 256], P('chan'), may hold values from -0.5 to 0.5
- channel_embed: bfloat16 [32, 256], P('chan'), may hold values from -6 to 6
- agg_query: float32 [256], replicated, may hold values from -160 to 160
- norm_gains: float32 [5, 256], replicated, may hold values from 0.25 to 1.75
- qkv_weight: bfloat16 [2, 256, 768], P(None, None, 'lon'), may hold values from -0.375 to 0.375
- proj_weight: bfloat16 [2, 256, 256], P(None, 'lon'), may hold values from -0.375 to 0.375
- up_weight: bfloat16 [2, 256, 1024], P(None, None, 'lon'), may hold values from -0.375 to 0.375
- down_weight: bfloat16 [2, 1024, 256], P(None, 'lon'), may hold values from -0.1875 to 0.1875
- decode_weight: bfloat16 [32, 256, 128], P('chan'), may hold values from -0.375 to 0.375
Outputs:
- decoded: bfloat16 [32, 128, 256, 128], P('chan', None, 'lon')
The draws below stay inside these ranges and needn't reach their ends.
All inputs are finite; a program needn't handle non-finite values.
Results may differ from the reference program's by a relative error of at most 0.018.
Values may be sent and summed in bfloat16 or wider, within the bound.
No kernel may reach another device: no remote copies, remote signals or barrier semaphores. Data moves between devices by JAX's collectives and lax.ppermute only.
A program may use at most 64 MiB of HBM per device.

```python
import jax
import jax.numpy as jnp
from jax import lax

C = 32
P_SIZE = 128
E = 256
H = 1024
HEADS = 8
WR = 8
WC = 8
ROWS = 128
LONS = 256


def draw_agg_query(key, part):
    base = jnp.clip(jax.random.normal(key, (E,), jnp.float32), -4.0, 4.0)
    return base


def block_levels(rng, shape, cuts, least, top_value):
    loudness, own = 1.0, jax.random.fold_in(rng, 6)
    for axis_at, shards_of in cuts:
        draws = jnp.exp(jax.random.uniform(jax.random.fold_in(own, axis_at), (shards_of,), jnp.float32, least / len(cuts), top_value / len(cuts)))
        loudness = loudness * jnp.repeat(draws, shape[axis_at] // shards_of).reshape([-1 if axis == axis_at else 1 for axis in range(len(shape))])
    return loudness


def bell_draw(key, dims, deviation, bound, split=(), kind=jnp.bfloat16):
    level = block_levels(key, dims, split, -0.22, 0.18) if split else 1.0
    array = jax.random.normal(key, dims, jnp.float32) * deviation * level
    return jnp.minimum(jnp.maximum(array, -bound), bound).astype(kind)


def setup_inputs(seed: int = 0) -> dict:
    key_of = jax.random.split(jax.random.key(seed), 11)
    patches = bell_draw(key_of[0], (C, ROWS, LONS, P_SIZE), 1.0, 6.0, ((0, 16), (2, 32)))
    embed_weight = bell_draw(key_of[1], (C, P_SIZE, E), P_SIZE ** -0.5, 0.5, ((0, 16),))
    channel_embed = bell_draw(key_of[2], (C, E), 1.0, 6.0, ((0, 16),))
    agg_query = draw_agg_query(jax.random.fold_in(key_of[10], 71), 0)
    norm_gains = jnp.clip(1.0 + 0.15 * jax.random.normal(key_of[4], (5, E), jnp.float32), 0.25, 1.75)
    qkv_weight = bell_draw(key_of[5], (2, E, 3 * E), E ** -0.5, 0.375, ((2, 32),))
    proj_weight = bell_draw(key_of[6], (2, E, E), E ** -0.5, 0.375, ((1, 32),))
    up_weight = bell_draw(key_of[7], (2, E, H), E ** -0.5, 0.375, ((2, 32),))
    down_weight = bell_draw(key_of[8], (2, H, E), H ** -0.5, 0.1875, ((1, 32),))
    decode_weight = bell_draw(key_of[9], (C, E, P_SIZE), E ** -0.5, 0.375, ((0, 16),))
    return {"patches": patches, "embed_weight": embed_weight, "channel_embed": channel_embed, "agg_query": agg_query, "norm_gains": norm_gains, "qkv_weight": qkv_weight, "proj_weight": proj_weight, "up_weight": up_weight, "down_weight": down_weight, "decode_weight": decode_weight}


EPS = 1e-05

def layer_norm(values, gain):
    mean = lax.optimization_barrier(jnp.mean(values, axis=-1, keepdims=True))
    centred = values - mean
    spread = lax.optimization_barrier(jnp.mean(centred * centred, axis=-1, keepdims=True))
    return centred * lax.rsqrt(spread + EPS) * gain

def window_block(windows, gain_attn, gain_mlp, w_qkv, w_proj, w_up, w_down):
    count, length, width = windows.shape
    head_dim = width // HEADS
    flat = windows.reshape(count * length, width)
    normed = layer_norm(flat, gain_attn).astype(jnp.bfloat16)
    qkv = jnp.dot(normed, w_qkv, preferred_element_type=jnp.float32).astype(jnp.bfloat16)
    qkv = lax.optimization_barrier(qkv)
    qkv = qkv.reshape(count, length, 3, HEADS, head_dim).astype(jnp.float32)
    scores = jnp.einsum('nqhd,nkhd->nhqk', qkv[:, :, 0], qkv[:, :, 1]) * head_dim ** (-0.5)
    probs = jax.nn.softmax(scores, axis=-1).astype(jnp.bfloat16)
    probs = lax.optimization_barrier(probs).astype(jnp.float32)
    mixed = jnp.einsum('nhqk,nkhd->nqhd', probs, qkv[:, :, 2]).astype(jnp.bfloat16)
    mixed = mixed.reshape(count * length, width)
    state = flat + jnp.dot(mixed, w_proj, preferred_element_type=jnp.float32)
    normed = layer_norm(state, gain_mlp).astype(jnp.bfloat16)
    hidden = jax.nn.gelu(jnp.dot(normed, w_up, preferred_element_type=jnp.float32)).astype(jnp.bfloat16)
    state = state + jnp.dot(hidden, w_down, preferred_element_type=jnp.float32)
    return state.reshape(count, length, width)

def apply_block(grid, layer, offset, norm_gains, qkv_weight, proj_weight, up_weight, down_weight):
    rows, cols, width = grid.shape
    rolled = jnp.roll(grid, -offset, axis=1)
    windows = rolled.reshape(rows // WR, WR, cols // WC, WC, width).transpose(0, 2, 1, 3, 4)
    windows = windows.reshape(-1, WR * WC, width)
    result = window_block(windows, norm_gains[2 * layer], norm_gains[2 * layer + 1], qkv_weight[layer], proj_weight[layer], up_weight[layer], down_weight[layer])
    result = result.reshape(rows // WR, cols // WC, WR, WC, width).transpose(0, 2, 1, 3, 4)
    return jnp.roll(result.reshape(rows, cols, width), offset, axis=1)

def reference(patches, embed_weight, channel_embed, agg_query, norm_gains, qkv_weight, proj_weight, up_weight, down_weight, decode_weight):
    count = ROWS * LONS
    flat = patches.reshape(C, count, P_SIZE)
    query_proj = jnp.einsum('cpe,e->cp', embed_weight.astype(jnp.float32), agg_query, precision=lax.Precision.HIGHEST)
    bias_score = jnp.dot(channel_embed.astype(jnp.float32), agg_query, precision=lax.Precision.HIGHEST)

    def channel_score(index):
        piece = flat[index].astype(jnp.float32)
        return jnp.dot(piece, query_proj[index], precision=lax.Precision.HIGHEST) + bias_score[index]
    scores = lax.map(channel_score, jnp.arange(C, dtype=jnp.int32)) * E ** (-0.5)
    top = lax.optimization_barrier(jnp.max(scores, axis=0))
    shares = jnp.exp(scores - top[None])
    denom = lax.optimization_barrier(jnp.sum(shares, axis=0))

    def accumulate(total, index):
        embedded = jnp.dot(flat[index], embed_weight[index], preferred_element_type=jnp.float32)
        embedded = embedded + channel_embed[index].astype(jnp.float32)[None]
        return (total + shares[index][:, None] * embedded, None)
    numer, _ = lax.scan(accumulate, jnp.zeros((count, E), jnp.float32), jnp.arange(C, dtype=jnp.int32))
    grid = (numer / denom[:, None]).reshape(ROWS, LONS, E)
    grid = apply_block(grid, 0, 0, norm_gains, qkv_weight, proj_weight, up_weight, down_weight)
    grid = apply_block(grid, 1, WC // 2, norm_gains, qkv_weight, proj_weight, up_weight, down_weight)
    final = layer_norm(grid.reshape(count, E), norm_gains[4]).astype(jnp.bfloat16)

    def decode(index):
        return jnp.dot(final, decode_weight[index], preferred_element_type=jnp.float32).astype(jnp.bfloat16)
    decoded = lax.map(decode, jnp.arange(C, dtype=jnp.int32))
    return decoded.reshape(C, ROWS, LONS, P_SIZE)
```

```python
import functools

import jax
import jax.numpy as jnp
from jax import lax
from jax.experimental import pallas as pl
from jax.experimental.pallas import tpu as pltpu
from jax.sharding import Mesh, PartitionSpec as P

HEADS = 8
WC = 8
EPS = 1e-05
F32 = jnp.float32
BF16 = jnp.bfloat16
GROUP = ("y", "core")
RING = ("zh", "zl")
EXTRA = 16


def dot_nt(a, b):
    return lax.dot_general(a, b, (((1,), (1,)), ((), ())), preferred_element_type=F32)


def dot_nn(a, b):
    return lax.dot_general(a, b, (((1,), (0,)), ((), ())), preferred_element_type=F32)


def thirds(x):
    hi = x.astype(BF16).astype(F32)
    mid = (x - hi).astype(BF16).astype(F32)
    return hi, mid, (x - hi) - mid


def in_rows(rows, count):
    at = lax.broadcasted_iota(jnp.int32, (count, rows[0].shape[1]), 0)
    out = jnp.zeros((count, rows[0].shape[1]), F32)
    for k, row in enumerate(rows):
        out = jnp.where(at == k, row, out)
    return out


def columns_of(rows):
    n = rows.shape[0]
    full = jnp.concatenate([rows, jnp.zeros((128 - n, 128), F32)], axis=0)
    return full.T


def embed_kernel(patches, weight, chan, query, out):
    tokens = patches.shape[1]
    own = tokens // out.shape[0]
    q = query[...]
    parts = in_rows(thirds(q), 16).astype(BF16)
    scale = q.shape[1] ** (-0.5)
    scores = []
    for c in range(2):
        proj = jnp.sum(dot_nt(parts, weight[c]), axis=0, keepdims=True)
        bias = jnp.sum(chan[c : c + 1, :].astype(F32) * q, axis=1, keepdims=True)
        split = in_rows(thirds(proj), 16).astype(BF16)
        terms = dot_nt(split, patches[c])
        scores.append((jnp.sum(terms, axis=0, keepdims=True) + bias) * scale)
    top = jnp.maximum(scores[0], scores[1])
    first = jnp.exp(scores[0] - top)
    total = first + jnp.exp(scores[1] - top)
    share = first / total
    extra = in_rows(thirds(top) + thirds(total), EXTRA).astype(BF16)
    chan0 = chan[0:1, :].astype(F32)
    chan1 = chan[1:2, :].astype(F32)
    for j in range(out.shape[0]):
        lo, hi = j * own, (j + 1) * own
        e0 = dot_nn(patches[0, lo:hi, :], weight[0]) + chan0
        e1 = dot_nn(patches[1, lo:hi, :], weight[1]) + chan1
        w = jnp.broadcast_to(share[:, lo:hi], (own, own)).T
        w = jnp.concatenate([w, w], axis=1)
        out[j, :own, :] = (e1 + w * (e0 - e1)).astype(BF16)
        out[j, own:, :own] = extra[:, lo:hi]
        out[j, own:, own:] = jnp.zeros((EXTRA, out.shape[2] - own), BF16)


def top_and_total(block):
    x = block.astype(F32)
    return x[0:1] + (x[1:2] + x[2:3]), x[3:4] + (x[4:5] + x[5:6])


def merged(averages, tops, totals):
    top = functools.reduce(jnp.maximum, tops)
    shares = [t * jnp.exp(m - top) for m, t in zip(tops, totals)]
    total = functools.reduce(jnp.add, shares)
    weights = columns_of(in_rows([s / total for s in shares], 8))
    out = None
    for d, average in enumerate(averages):
        term = weights[:, d : d + 1] * average
        out = term if out is None else out + term
    return out, top, total


def combine_kernel(got, sent, own, own_rows):
    count = got.shape[0]
    n = own.shape[0]
    stats = [top_and_total(got[d, n:, :n]) for d in range(count)]
    averages = [got[d, :n, :].astype(F32) for d in range(count)]
    state, top, total = merged(averages, [s[0] for s in stats], [s[1] for s in stats])
    own[...] = state
    own_rows[...] = in_rows([top, total], 8)
    sent[:n, :] = state.astype(BF16)
    sent[n:, :n] = in_rows(thirds(top) + thirds(total), EXTRA).astype(BF16)
    sent[n:, n:] = jnp.zeros((EXTRA, sent.shape[1] - n), BF16)


def norm(v, gain):
    mean = jnp.mean(v, axis=-1, keepdims=True)
    centred = v - mean
    spread = jnp.mean(centred * centred, axis=-1, keepdims=True)
    return centred * lax.rsqrt(spread + EPS) * gain


def attention_weights(layer, mine, other, qkv_rows, proj_rows):
    first_core = lax.axis_index("core") == 0
    x_at, zl_at = lax.axis_index("x"), lax.axis_index("zl")
    lo = 48 * layer
    for xs in range(4):
        for slot, back in enumerate(ZL_BACK):
            lon = ((x_at + (4 - xs)) & 3) * 8 + ((zl_at + (16 - back)) & 7)
            piece = xs * 8 + slot
            a = mine[piece, lo : lo + 16, :].astype(F32)
            b = other[piece, lo : lo + 16, :].astype(F32)
            head = jnp.where(first_core, a, b)
            tail = jnp.where(first_core, b, a)
            at = pl.multiple_of(lon * 24, 8)
            qkv_rows[pl.ds(at, 16), :] = head
            qkv_rows[pl.ds(at + 16, 8), :] = tail[:8]
            proj_rows[pl.ds(pl.multiple_of(lon * 8, 8), 8), :] = tail[8:]
    return qkv_rows[...].astype(BF16), proj_rows[...].astype(BF16)


def mlp_weights(layer, mine, other):
    lo = 48 * layer
    width = mine.shape[2]

    def rows(at):
        return jnp.concatenate(
            [w[:, at : at + 16, :].reshape(-1, width) for w in (mine, other)], axis=0
        )

    return rows(lo + 16), rows(lo + 32)


def attend(q, keys, values, allowed):
    width = q.shape[1]
    per_head = width // HEADS
    scale = per_head ** (-0.5)
    lane_head = lax.broadcasted_iota(jnp.int32, keys.shape, 1) // per_head
    mixed = None
    for h in range(HEADS):
        here = lane_head == h
        k = jnp.where(here, keys, 0.0).astype(BF16)
        v = jnp.where(here, values, 0.0).astype(BF16)
        s = jnp.where(allowed, dot_nt(q, k) * scale, -jnp.inf)
        e = jnp.exp(s - jnp.max(s, axis=1, keepdims=True))
        p = (e / jnp.sum(e, axis=1, keepdims=True)).astype(BF16)
        part = dot_nn(p, v)
        mixed = part if mixed is None else mixed + part
    return mixed.astype(BF16)


def gelu(x):
    return jax.nn.gelu(x, approximate=True)


def after_attention(x, mixed, gain, w_proj, w_up, w_down):
    x1 = x + dot_nn(mixed, w_proj)
    normed = norm(x1, gain).astype(BF16)
    hidden = gelu(dot_nt(normed, w_up)).astype(BF16)
    return x1 + dot_nn(hidden, w_down)


def token_at(shape, dim):
    t = lax.broadcasted_iota(jnp.int32, shape, dim)
    return t // 64, (t & 7) // 4, t


def half_tokens(x, half):
    to = lax.broadcasted_iota(jnp.int32, (64, 128), 0)
    source = lax.broadcasted_iota(jnp.int32, (64, 128), 1)
    pick = (to // 4) * 8 + half * 4 + (to & 3) == source
    return dot_nn(jnp.where(pick, 1.0, 0.0).astype(BF16), x).astype(BF16)


def block0_kernel(own, own_rows, got, gains, mine, other, state, west, east, qkv_rows, proj_rows):
    n, width = own.shape
    got_top, got_total = top_and_total(got[n:, :n])
    rows = own_rows[...]
    x, _, _ = merged(
        [own[...], got[:n, :].astype(F32)], [rows[0:1], got_top], [rows[1:2], got_total]
    )
    w_qkv, w_proj = attention_weights(0, mine, other, qkv_rows, proj_rows)
    w_up, w_down = mlp_weights(0, mine, other)
    a = norm(x, gains[0:1, :]).astype(BF16)
    qkv = dot_nt(a, w_qkv).astype(BF16).astype(F32)
    allowed = token_at((n, n), 0)[0] == token_at((n, n), 1)[0]
    mixed = attend(
        qkv[:, :width].astype(BF16), qkv[:, width : 2 * width], qkv[:, 2 * width :], allowed
    )
    x = after_attention(x, mixed, gains[1:2, :], w_proj, w_up, w_down)
    state[...] = x
    short = x.astype(BF16)
    west[...] = half_tokens(short, 0)
    east[...] = half_tokens(short, 1)


def block1_kernel(state, from_west, from_east, gains, mine, other, out, qkv_rows, proj_rows):
    n, width = state.shape
    x = state[...]
    w_qkv, w_proj = attention_weights(1, mine, other, qkv_rows, proj_rows)
    w_up, w_down = mlp_weights(1, mine, other)
    sides = jnp.concatenate([from_west[...].astype(F32), from_east[...].astype(F32)], axis=0)
    gain = gains[2:3, :]
    a = norm(x, gain).astype(BF16)
    b = norm(sides, gain).astype(BF16)
    qkv = dot_nt(a, w_qkv).astype(BF16).astype(F32)
    side_kv = dot_nt(b, w_qkv[width:, :]).astype(BF16).astype(F32)
    keys = jnp.concatenate([qkv[:, width : 2 * width], side_kv[:, :width]], axis=0)
    values = jnp.concatenate([qkv[:, 2 * width :], side_kv[:, width:]], axis=0)
    q_block, q_half, _ = token_at((n, 2 * n), 0)
    k_block, k_half, k_at = token_at((n, 2 * n), 1)
    side = k_at - n
    k_block = jnp.where(k_at < n, k_block, (side & 63) // 32)
    k_half = jnp.where(k_at < n, k_half, side // 64)
    allowed = (q_block == k_block) & (q_half == k_half)
    mixed = attend(qkv[:, :width].astype(BF16), keys, values, allowed)
    x = after_attention(x, mixed, gains[3:4, :], w_proj, w_up, w_down)
    final = norm(x, gains[4:5, :]).astype(BF16)
    for j in range(out.shape[0]):
        out[j] = final


def decode_kernel(tokens, weight, out):
    count, own, width = tokens.shape
    for c in range(2):
        w = weight[c]
        for j in range(count):
            out[c, j * own : (j + 1) * own, :] = dot_nn(tokens[j], w).astype(BF16)


def on_core(kernel, outs, scratch=(), flops=0, moved=0):
    vmem = pl.BlockSpec(memory_space=pltpu.VMEM)

    def call(*operands):
        return pl.pallas_call(
            kernel,
            out_shape=outs,
            in_specs=[vmem] * len(operands),
            out_specs=jax.tree.map(lambda _: vmem, outs),
            scratch_shapes=list(scratch),
            compiler_params=pltpu.CompilerParams(vmem_limit_bytes=40 * 2**20),
            cost_estimate=pl.CostEstimate(flops=flops, bytes_accessed=moved, transcendentals=0),
        )(*operands)

    return call


def shifted(value, axes, size, steps):
    return lax.ppermute(value, axes, [(i, (i + steps) % size) for i in range(size)])


ZL_BACK = (0, 2, -2, 4, 1, 3, -1, 5)


def eastward():
    pairs = []
    for zh in range(2):
        for x in range(4):
            for zl in range(8):
                to = (zh, x, zl + 1) if zl < 7 else (1 - zh, (x + 1) % 4, 0)
                pairs.append(((zh * 4 + x) * 8 + zl, (to[0] * 4 + to[1]) * 8 + to[2]))
    return pairs


def weight_pieces(qkv, proj, up, down):
    core = lax.axis_index("core")
    qkv, up = jnp.swapaxes(qkv, 1, 2), jnp.swapaxes(up, 1, 2)
    attn = jnp.concatenate([qkv, proj], axis=1)
    lanes = [lax.dynamic_slice_in_dim(a, core * 16, 16, 1) for a in (attn, up, down)]
    piece = jnp.concatenate(lanes, axis=1)
    return piece.reshape(1, -1, piece.shape[2])


def body(
    patches,
    embed_weight,
    channel_embed,
    agg_query,
    norm_gains,
    qkv_weight,
    proj_weight,
    up_weight,
    down_weight,
    decode_weight,
):
    chans, rows, cols, width_p = patches.shape
    width = embed_weight.shape[2]
    tokens = rows * cols
    parts = lax.axis_size("y") * lax.axis_size("core")
    own = tokens // parts

    piece = weight_pieces(qkv_weight, proj_weight, up_weight, down_weight)
    pieces = jnp.concatenate(
        [piece] + [shifted(piece, RING, 16, k) for k in (2, -2, 4)], axis=0
    )
    pieces = jnp.concatenate([pieces, shifted(pieces, RING, 16, 1)], axis=0)
    mine = jnp.concatenate([pieces] + [shifted(pieces, "x", 4, k) for k in (1, 2, 3)], axis=0)
    other = shifted(mine, "core", 2, 1)

    sums = on_core(
        embed_kernel,
        jax.ShapeDtypeStruct((parts, own + EXTRA, width), BF16),
        flops=2 * chans * tokens * width_p * width,
        moved=2 * 2**20,
    )(
        patches.reshape(chans, tokens, width_p),
        embed_weight,
        channel_embed,
        agg_query.reshape(1, width),
    )
    got = lax.all_to_all(sums, GROUP, 0, 0, tiled=True)
    sent, average, stats = on_core(
        combine_kernel,
        (
            jax.ShapeDtypeStruct((own + EXTRA, width), BF16),
            jax.ShapeDtypeStruct((own, width), F32),
            jax.ShapeDtypeStruct((8, own), F32),
        ),
        moved=2**20,
    )(got)
    partner = shifted(sent, "zh", 2, 1)

    scratch = [pltpu.VMEM((3 * width, width), F32), pltpu.VMEM((width, width), F32)]
    half = jax.ShapeDtypeStruct((own // 2, width), BF16)
    block_flops = 2 * own * width * width * 12
    state, west, east = on_core(
        block0_kernel,
        (jax.ShapeDtypeStruct((own, width), F32), half, half),
        scratch,
        flops=block_flops,
        moved=4 * 2**20,
    )(average, stats, partner, norm_gains, mine, other)
    pairs = eastward()
    from_west = lax.ppermute(east, ("zh", "x", "zl"), pairs)
    from_east = lax.ppermute(west, ("zh", "x", "zl"), [(b, a) for a, b in pairs])
    final = on_core(
        block1_kernel,
        jax.ShapeDtypeStruct((parts, own, width), BF16),
        scratch,
        flops=block_flops,
        moved=4 * 2**20,
    )(state, from_west, from_east, norm_gains, mine, other)
    everyone = lax.all_to_all(final, GROUP, 0, 0, tiled=True)
    decoded = on_core(
        decode_kernel,
        jax.ShapeDtypeStruct((chans, tokens, width_p), BF16),
        flops=2 * chans * tokens * width_p * width,
        moved=2 * 2**20,
    )(everyone, decode_weight)
    return decoded.reshape(chans, rows, cols, width_p)


def solution(mesh):
    fine = Mesh(mesh.devices.reshape(2, 4, 2, 4, 8), ("zh", "y", "core", "x", "zl"))
    chan, lon = ("zh", "y", "core"), ("x", "zl")
    placed = (
        P(chan, None, lon, None),
        P(chan, None, None),
        P(chan, None),
        P(),
        P(),
        P(None, None, lon),
        P(None, lon, None),
        P(None, None, lon),
        P(None, lon, None),
        P(chan, None, None),
    )
    return jax.shard_map(
        body, mesh=fine, in_specs=placed, out_specs=P(chan, None, lon, None), check_vma=False
    )
```

```python
import functools

import jax
import jax.numpy as jnp
from jax import lax
from jax.experimental import pallas as pl
from jax.experimental.pallas import tpu as pltpu
from jax.sharding import Mesh, PartitionSpec as P

HEADS = 8
WC = 8
EPS = 1e-05
F32 = jnp.float32
BF16 = jnp.bfloat16
GROUP = ("y", "core")
EXTRA = 16


def dot_nt(a, b):
    return lax.dot_general(a, b, (((1,), (1,)), ((), ())), preferred_element_type=F32)


def dot_nn(a, b):
    return lax.dot_general(a, b, (((1,), (0,)), ((), ())), preferred_element_type=F32)


def thirds(x):
    hi = x.astype(BF16).astype(F32)
    mid = (x - hi).astype(BF16).astype(F32)
    return hi, mid, (x - hi) - mid


def in_rows(rows, count):
    at = lax.broadcasted_iota(jnp.int32, (count, rows[0].shape[1]), 0)
    out = jnp.zeros((count, rows[0].shape[1]), F32)
    for k, row in enumerate(rows):
        out = jnp.where(at == k, row, out)
    return out


def columns_of(rows):
    n = rows.shape[0]
    full = jnp.concatenate([rows, jnp.zeros((128 - n, 128), F32)], axis=0)
    return full.T


def embed_kernel(patches, weight, chan, query, *outs):
    tokens = patches.shape[1]
    owners = 2 * outs[0].shape[0]
    own = tokens // owners
    q = query[...]
    parts = in_rows(thirds(q), 16).astype(BF16)
    scale = q.shape[1] ** (-0.5)
    scores = []
    for c in range(2):
        proj = jnp.sum(dot_nt(parts, weight[c]), axis=0, keepdims=True)
        bias = jnp.sum(chan[c : c + 1, :].astype(F32) * q, axis=1, keepdims=True)
        split = in_rows(thirds(proj), 16).astype(BF16)
        terms = dot_nt(split, patches[c])
        scores.append((jnp.sum(terms, axis=0, keepdims=True) + bias) * scale)
    top = jnp.maximum(scores[0], scores[1])
    first = jnp.exp(scores[0] - top)
    total = first + jnp.exp(scores[1] - top)
    share = first / total
    extra = in_rows(thirds(top) + thirds(total), EXTRA).astype(BF16)
    chan0 = chan[0:1, :].astype(F32)
    chan1 = chan[1:2, :].astype(F32)
    for j in range(owners):
        lo, hi = j * own, (j + 1) * own
        e0 = dot_nn(patches[0, lo:hi, :], weight[0]) + chan0
        e1 = dot_nn(patches[1, lo:hi, :], weight[1]) + chan1
        w = jnp.broadcast_to(share[:, lo:hi], (own, own)).T
        w = jnp.concatenate([w, w], axis=1)
        out = outs[j % 2]
        out[j // 2, :own, :] = (e1 + w * (e0 - e1)).astype(BF16)
        out[j // 2, own:, :own] = extra[:, lo:hi]
        out[j // 2, own:, own:] = jnp.zeros((EXTRA, out.shape[2] - own), BF16)


def top_and_total(block):
    x = block.astype(F32)
    return x[0:1] + (x[1:2] + x[2:3]), x[3:4] + (x[4:5] + x[5:6])


def merged(averages, tops, totals):
    top = functools.reduce(jnp.maximum, tops)
    shares = [t * jnp.exp(m - top) for m, t in zip(tops, totals)]
    total = functools.reduce(jnp.add, shares)
    weights = columns_of(in_rows([s / total for s in shares], 8))
    out = None
    for d, average in enumerate(averages):
        term = weights[:, d : d + 1] * average
        out = term if out is None else out + term
    return out, top, total


def put_message(out, state, top, total):
    n = state.shape[0]
    out[:n, :] = state.astype(BF16)
    out[n:, :n] = in_rows(thirds(top) + thirds(total), EXTRA).astype(BF16)
    out[n:, n:] = jnp.zeros((EXTRA, out.shape[1] - n), BF16)


def merge_messages(messages):
    n = messages[0].shape[0] - EXTRA
    stats = [top_and_total(m[n:, :n]) for m in messages]
    averages = [m[:n, :].astype(F32) for m in messages]
    return merged(averages, [s[0] for s in stats], [s[1] for s in stats])


def pair_kernel(first, second, got, *outs):
    core, y = lax.axis_index("core"), lax.axis_index("y")
    for k, out in enumerate(outs):
        to = (y + k) & 3
        mine = jnp.where(core == 0, first[to].astype(F32), second[to].astype(F32))
        put_message(out, *merge_messages([mine, got[to]]))


def combine_kernel(mine, one, two, three, sent, own, own_rows):
    state, top, total = merge_messages([m[...] for m in (mine, one, two, three)])
    own[...] = state
    own_rows[...] = in_rows([top, total], 8)
    put_message(sent, state, top, total)


def norm(v, gain):
    mean = jnp.mean(v, axis=-1, keepdims=True)
    centred = v - mean
    spread = jnp.mean(centred * centred, axis=-1, keepdims=True)
    return centred * lax.rsqrt(spread + EPS) * gain


def attention_weights(layer, mine, other, qkv_rows, proj_rows):
    lo = 48 * layer
    first_core = lax.axis_index("core") == 0
    for lon in range(mine.shape[0]):
        a = mine[lon, lo : lo + 16, :].astype(F32)
        b = other[lon, lo : lo + 16, :].astype(F32)
        tail = jnp.where(first_core, b, a)
        qkv_rows[lon * 24 : lon * 24 + 16, :] = jnp.where(first_core, a, b)
        qkv_rows[lon * 24 + 16 : lon * 24 + 24, :] = tail[:8]
        proj_rows[lon * 8 : lon * 8 + 8, :] = tail[8:]
    return qkv_rows[...].astype(BF16), proj_rows[...].astype(BF16)


def mlp_weights(layer, mine, other):
    lo = 48 * layer
    width = mine.shape[2]

    def rows(at):
        return jnp.concatenate(
            [w[:, at : at + 16, :].reshape(-1, width) for w in (mine, other)], axis=0
        )

    return rows(lo + 16), rows(lo + 32)


def attend(q, keys, values, allowed):
    width = q.shape[1]
    per_head = width // HEADS
    scale = per_head ** (-0.5)
    lane_head = lax.broadcasted_iota(jnp.int32, keys.shape, 1) // per_head
    mixed = None
    for h in range(HEADS):
        here = lane_head == h
        k = jnp.where(here, keys, 0.0).astype(BF16)
        v = jnp.where(here, values, 0.0).astype(BF16)
        s = jnp.where(allowed, dot_nt(q, k) * scale, -jnp.inf)
        e = jnp.exp(s - jnp.max(s, axis=1, keepdims=True))
        p = (e / jnp.sum(e, axis=1, keepdims=True)).astype(BF16)
        part = dot_nn(p, v)
        mixed = part if mixed is None else mixed + part
    return mixed.astype(BF16)


def gelu(x):
    return jax.nn.gelu(x, approximate=True)


def after_attention(x, mixed, gain, w_proj, w_up, w_down):
    x1 = x + dot_nn(mixed, w_proj)
    normed = norm(x1, gain).astype(BF16)
    hidden = gelu(dot_nt(normed, w_up)).astype(BF16)
    return x1 + dot_nn(hidden, w_down)


def token_at(shape, dim):
    t = lax.broadcasted_iota(jnp.int32, shape, dim)
    return t // 64, (t & 7) // 4, t


def half_tokens(x, half):
    to = lax.broadcasted_iota(jnp.int32, (64, 128), 0)
    source = lax.broadcasted_iota(jnp.int32, (64, 128), 1)
    pick = (to // 4) * 8 + half * 4 + (to & 3) == source
    return dot_nn(jnp.where(pick, 1.0, 0.0).astype(BF16), x).astype(BF16)


def block0_kernel(own, own_rows, got, gains, mine, other, state, west, east, qkv_rows, proj_rows):
    n, width = own.shape
    got_top, got_total = top_and_total(got[n:, :n])
    rows = own_rows[...]
    x, _, _ = merged(
        [own[...], got[:n, :].astype(F32)], [rows[0:1], got_top], [rows[1:2], got_total]
    )
    w_qkv, w_proj = attention_weights(0, mine, other, qkv_rows, proj_rows)
    w_up, w_down = mlp_weights(0, mine, other)
    a = norm(x, gains[0:1, :]).astype(BF16)
    qkv = dot_nt(a, w_qkv).astype(BF16).astype(F32)
    allowed = token_at((n, n), 0)[0] == token_at((n, n), 1)[0]
    mixed = attend(
        qkv[:, :width].astype(BF16), qkv[:, width : 2 * width], qkv[:, 2 * width :], allowed
    )
    x = after_attention(x, mixed, gains[1:2, :], w_proj, w_up, w_down)
    state[...] = x
    short = x.astype(BF16)
    west[...] = half_tokens(short, 0)
    east[...] = half_tokens(short, 1)


def block1_kernel(state, from_west, from_east, gains, mine, other, out, qkv_rows, proj_rows):
    n, width = state.shape
    x = state[...]
    w_qkv, w_proj = attention_weights(1, mine, other, qkv_rows, proj_rows)
    w_up, w_down = mlp_weights(1, mine, other)
    sides = jnp.concatenate([from_west[...].astype(F32), from_east[...].astype(F32)], axis=0)
    gain = gains[2:3, :]
    a = norm(x, gain).astype(BF16)
    b = norm(sides, gain).astype(BF16)
    qkv = dot_nt(a, w_qkv).astype(BF16).astype(F32)
    side_kv = dot_nt(b, w_qkv[width:, :]).astype(BF16).astype(F32)
    keys = jnp.concatenate([qkv[:, width : 2 * width], side_kv[:, :width]], axis=0)
    values = jnp.concatenate([qkv[:, 2 * width :], side_kv[:, width:]], axis=0)
    q_block, q_half, _ = token_at((n, 2 * n), 0)
    k_block, k_half, k_at = token_at((n, 2 * n), 1)
    side = k_at - n
    k_block = jnp.where(k_at < n, k_block, (side & 63) // 32)
    k_half = jnp.where(k_at < n, k_half, side // 64)
    allowed = (q_block == k_block) & (q_half == k_half)
    mixed = attend(qkv[:, :width].astype(BF16), keys, values, allowed)
    x = after_attention(x, mixed, gains[3:4, :], w_proj, w_up, w_down)
    final = norm(x, gains[4:5, :]).astype(BF16)
    for j in range(out.shape[0]):
        out[j] = final


def decode_kernel(tokens, weight, out):
    count, own, width = tokens.shape
    for c in range(2):
        w = weight[c]
        for j in range(count):
            out[c, j * own : (j + 1) * own, :] = dot_nn(tokens[j], w).astype(BF16)


def spread_kernel(count, times, *refs):
    parts, outs = refs[:count], refs[-len(times) :]
    height = outs[0].shape[-2]
    at = 0
    for part in parts:
        n = part.shape[0]
        for layer, (out, repeat) in enumerate(zip(outs, times)):
            rows = part[:, layer * height : (layer + 1) * height, :]
            for k in range(repeat):
                out[k, at : at + n] = rows
        at += n


def spread(parts, times, after=()):
    pieces, height, width = parts[0].shape
    total = sum(p.shape[0] for p in parts)
    vmem, anywhere = pl.BlockSpec(memory_space=pltpu.VMEM), pl.BlockSpec(memory_space=pl.ANY)
    return pl.pallas_call(
        functools.partial(spread_kernel, len(parts), times),
        out_shape=[
            jax.ShapeDtypeStruct((n, total, height // len(times), width), BF16) for n in times
        ],
        in_specs=[vmem] * len(parts) + [anywhere] * len(after),
        out_specs=[vmem] * len(times),
        compiler_params=pltpu.CompilerParams(vmem_limit_bytes=16 * 2**20),
        cost_estimate=pl.CostEstimate(
            flops=0, bytes_accessed=2 * (1 + sum(times)) * total * height * width, transcendentals=0
        ),
    )(*parts, *after)


def held_until(value, after):
    anywhere = pl.BlockSpec(memory_space=pl.ANY)
    return pl.pallas_call(
        lambda *refs: None,
        out_shape=jax.ShapeDtypeStruct(value.shape, value.dtype),
        in_specs=[anywhere] * (1 + len(after)),
        out_specs=anywhere,
        input_output_aliases={0: 0},
    )(value, *after)


def on_core(kernel, outs, scratch=(), flops=0, moved=0, after=()):
    vmem, anywhere = pl.BlockSpec(memory_space=pltpu.VMEM), pl.BlockSpec(memory_space=pl.ANY)

    def ordered(*refs):
        kernel(*refs[len(after) :])

    def call(*operands):
        return pl.pallas_call(
            ordered,
            out_shape=outs,
            in_specs=[anywhere] * len(after) + [vmem] * len(operands),
            out_specs=jax.tree.map(lambda _: vmem, outs),
            scratch_shapes=list(scratch),
            compiler_params=pltpu.CompilerParams(vmem_limit_bytes=40 * 2**20),
            cost_estimate=pl.CostEstimate(flops=flops, bytes_accessed=moved, transcendentals=0),
        )(*after, *operands)

    return call


def shifted(value, axes, size, steps):
    return lax.ppermute(value, axes, [(i, (i + steps) % size) for i in range(size)])


def eastward():
    pairs = []
    for zh in range(2):
        for x in range(4):
            for zl in range(8):
                to = (zh, x, zl + 1) if zl < 7 else (1 - zh, (x + 1) % 4, 0)
                pairs.append(((zh * 4 + x) * 8 + zl, (to[0] * 4 + to[1]) * 8 + to[2]))
    return pairs


def weight_pieces(qkv, proj, up, down):
    core = lax.axis_index("core")
    qkv, up = jnp.swapaxes(qkv, 1, 2), jnp.swapaxes(up, 1, 2)
    attn = jnp.concatenate([qkv, proj], axis=1)
    lanes = [lax.dynamic_slice_in_dim(a, core * 16, 16, 1) for a in (attn, up, down)]
    piece = jnp.concatenate(lanes, axis=1)
    return piece.reshape(1, -1, piece.shape[2])


def body(
    patches,
    embed_weight,
    channel_embed,
    agg_query,
    norm_gains,
    qkv_weight,
    proj_weight,
    up_weight,
    down_weight,
    decode_weight,
):
    chans, rows, cols, width_p = patches.shape
    width = embed_weight.shape[2]
    tokens = rows * cols
    parts = lax.axis_size("y") * lax.axis_size("core")
    own = tokens // parts

    piece = weight_pieces(qkv_weight, proj_weight, up_weight, down_weight)
    (near,) = spread([piece], (8,))
    near = lax.all_to_all(near.reshape(8, -1, width), "zl", 0, 0, tiled=True)

    message = jax.ShapeDtypeStruct((own + EXTRA, width), BF16)
    messages = jax.ShapeDtypeStruct((4, own + EXTRA, width), BF16)
    first, second = on_core(
        embed_kernel,
        (messages, messages),
        flops=2 * chans * tokens * width_p * width,
        moved=2 * 2**20,
    )(
        patches.reshape(chans, tokens, width_p),
        embed_weight,
        channel_embed,
        agg_query.reshape(1, width),
    )
    leaving = jnp.where(lax.axis_index("core") == 0, second, first)
    got = shifted(leaving, "core", 2, 1)
    paired = on_core(pair_kernel, (message,) * 4, moved=2**20)(first, second, got)
    along = [shifted(paired[k], "y", 4, k) for k in (1, 2, 3)]
    sent, average, stats = on_core(
        combine_kernel,
        (
            message,
            jax.ShapeDtypeStruct((own, width), F32),
            jax.ShapeDtypeStruct((8, own), F32),
        ),
        moved=2**20,
    )(paired[0], *along)
    (copies,) = spread([near], (4,), after=(sent,))
    mine = lax.all_to_all(copies, "x", 0, 0, tiled=True).reshape(32, -1, width)
    partner = shifted(sent, "zh", 2, 1)
    mine = held_until(mine, (partner,))
    other = shifted(mine, "core", 2, 1)

    scratch = [pltpu.VMEM((3 * width, width), F32), pltpu.VMEM((width, width), F32)]
    half = jax.ShapeDtypeStruct((own // 2, width), BF16)
    block_flops = 2 * own * width * width * 12
    state, west, east = on_core(
        block0_kernel,
        (jax.ShapeDtypeStruct((own, width), F32), half, half),
        scratch,
        flops=block_flops,
        moved=4 * 2**20,
    )(average, stats, partner, norm_gains, mine, other)
    pairs = eastward()
    from_west = lax.ppermute(east, ("zh", "x", "zl"), pairs)
    from_east = lax.ppermute(west, ("zh", "x", "zl"), [(b, a) for a, b in pairs])
    final = on_core(
        block1_kernel,
        jax.ShapeDtypeStruct((parts, own, width), BF16),
        scratch,
        flops=block_flops,
        moved=4 * 2**20,
    )(state, from_west, from_east, norm_gains, mine, other)
    everyone = lax.all_to_all(final, GROUP, 0, 0, tiled=True)
    decoded = on_core(
        decode_kernel,
        jax.ShapeDtypeStruct((chans, tokens, width_p), BF16),
        flops=2 * chans * tokens * width_p * width,
        moved=2 * 2**20,
    )(everyone, decode_weight)
    return decoded.reshape(chans, rows, cols, width_p)


def solution(mesh):
    fine = Mesh(mesh.devices.reshape(2, 4, 2, 4, 8), ("zh", "y", "core", "x", "zl"))
    chan, lon = ("zh", "y", "core"), ("x", "zl")
    placed = (
        P(chan, None, lon, None),
        P(chan, None, None),
        P(chan, None),
        P(),
        P(),
        P(None, None, lon),
        P(None, lon, None),
        P(None, None, lon),
        P(None, lon, None),
        P(chan, None, None),
    )
    return jax.shard_map(
        body, mesh=fine, in_specs=placed, out_specs=P(chan, None, lon, None), check_vma=False
    )
```

```python
import functools

import jax
import jax.numpy as jnp
from jax import lax
from jax.experimental import pallas as pl
from jax.experimental.pallas import tpu as pltpu
from jax.sharding import Mesh, PartitionSpec as P

HEADS = 8
WC = 8
EPS = 1e-05
F32 = jnp.float32
BF16 = jnp.bfloat16
GROUP = ("y", "core")
EXTRA = 16


def dot_nt(a, b):
    return lax.dot_general(a, b, (((1,), (1,)), ((), ())), preferred_element_type=F32)


def dot_nn(a, b):
    return lax.dot_general(a, b, (((1,), (0,)), ((), ())), preferred_element_type=F32)


def thirds(x):
    hi = x.astype(BF16).astype(F32)
    mid = (x - hi).astype(BF16).astype(F32)
    return hi, mid, (x - hi) - mid


def in_rows(rows, count):
    at = lax.broadcasted_iota(jnp.int32, (count, rows[0].shape[1]), 0)
    out = jnp.zeros((count, rows[0].shape[1]), F32)
    for k, row in enumerate(rows):
        out = jnp.where(at == k, row, out)
    return out


def columns_of(rows):
    n = rows.shape[0]
    full = jnp.concatenate([rows, jnp.zeros((128 - n, 128), F32)], axis=0)
    return full.T


def embed_kernel(table, patches, stay, leave, shares, extras):
    depth = patches.shape[2]
    weight = [table[c * depth : (c + 1) * depth, :].astype(BF16) for c in range(2)]
    chan = table[2 * depth : 2 * depth + 8, :]
    owners = 2 * stay.shape[0]
    own = patches.shape[1] // owners
    q = chan[2:3, :]
    parts = in_rows(thirds(q), 16).astype(BF16)
    scale = q.shape[1] ** (-0.5)
    scores = []
    for c in range(2):
        proj = jnp.sum(dot_nt(parts, weight[c]), axis=0, keepdims=True)
        bias = jnp.sum(chan[c : c + 1, :] * q, axis=1, keepdims=True)
        split = in_rows(thirds(proj), 16).astype(BF16)
        terms = dot_nt(split, patches[c])
        scores.append((jnp.sum(terms, axis=0, keepdims=True) + bias) * scale)
    top = jnp.maximum(scores[0], scores[1])
    first = jnp.exp(scores[0] - top)
    total = first + jnp.exp(scores[1] - top)
    shares[...] = in_rows((first / total,), 8)
    extras[...] = in_rows(thirds(top) + thirds(total), EXTRA)
    chan0, chan1 = chan[0:1, :], chan[1:2, :]
    core = lax.axis_index("core")
    for side, out in enumerate((stay, leave)):
        for y in range(out.shape[0]):
            at = pl.multiple_of((2 * y + (core ^ side)) * own, own)
            e0 = dot_nn(patches[0, pl.ds(at, own), :], weight[0]) + chan0
            e1 = dot_nn(patches[1, pl.ds(at, own), :], weight[1]) + chan1
            w = jnp.broadcast_to(shares[0:1, pl.ds(at, own)], (own, own)).T
            w = jnp.concatenate([w, w], axis=1)
            out[y, :own, :] = (e1 + w * (e0 - e1)).astype(BF16)
            out[y, own:, :own] = extras[:, pl.ds(at, own)].astype(BF16)
            out[y, own:, own:] = jnp.zeros((EXTRA, out.shape[2] - own), BF16)


def top_and_total(block):
    x = block.astype(F32)
    return x[0:1] + (x[1:2] + x[2:3]), x[3:4] + (x[4:5] + x[5:6])


def merged(averages, tops, totals):
    top = functools.reduce(jnp.maximum, tops)
    shares = [t * jnp.exp(m - top) for m, t in zip(tops, totals)]
    total = functools.reduce(jnp.add, shares)
    weights = columns_of(in_rows([s / total for s in shares], 8))
    out = None
    for d, average in enumerate(averages):
        term = weights[:, d : d + 1] * average
        out = term if out is None else out + term
    return out, top, total


def put_message(out, state, top, total):
    n = state.shape[0]
    out[:n, :] = state.astype(BF16)
    out[n:, :n] = in_rows(thirds(top) + thirds(total), EXTRA).astype(BF16)
    out[n:, n:] = jnp.zeros((EXTRA, out.shape[1] - n), BF16)


def merge_messages(messages):
    n = messages[0].shape[0] - EXTRA
    stats = [top_and_total(m[n:, :n]) for m in messages]
    averages = [m[:n, :].astype(F32) for m in messages]
    return merged(averages, [s[0] for s in stats], [s[1] for s in stats])


def pair_kernel(stay, got, *outs):
    y = lax.axis_index("y")
    for k, out in enumerate(outs):
        to = (y + k) & 3
        put_message(out, *merge_messages([stay[to], got[to]]))


def combine_kernel(mine, one, two, three, sent, own, own_rows):
    state, top, total = merge_messages([m[...] for m in (mine, one, two, three)])
    own[...] = state
    own_rows[...] = in_rows([top, total], 8)
    put_message(sent, state, top, total)


def norm(v, gain):
    mean = jnp.mean(v, axis=-1, keepdims=True)
    centred = v - mean
    spread = jnp.mean(centred * centred, axis=-1, keepdims=True)
    return centred * lax.rsqrt(spread + EPS) * gain


def attention_weights(layer, mine, other, qkv_rows, proj_rows):
    lo = 48 * layer
    first_core = lax.axis_index("core") == 0
    for lon in range(mine.shape[0]):
        a = mine[lon, lo : lo + 16, :].astype(F32)
        b = other[lon, lo : lo + 16, :].astype(F32)
        tail = jnp.where(first_core, b, a)
        qkv_rows[lon * 24 : lon * 24 + 16, :] = jnp.where(first_core, a, b)
        qkv_rows[lon * 24 + 16 : lon * 24 + 24, :] = tail[:8]
        proj_rows[lon * 8 : lon * 8 + 8, :] = tail[8:]
    return qkv_rows[...].astype(BF16), proj_rows[...].astype(BF16)


def mlp_weights(layer, mine, other):
    lo = 48 * layer
    width = mine.shape[2]

    def rows(at):
        return jnp.concatenate(
            [w[:, at : at + 16, :].reshape(-1, width) for w in (mine, other)], axis=0
        )

    return rows(lo + 16), rows(lo + 32)


def attend(q, keys, values, allowed):
    width = q.shape[1]
    per_head = width // HEADS
    scale = per_head ** (-0.5)
    lane_head = lax.broadcasted_iota(jnp.int32, keys.shape, 1) // per_head
    mixed = None
    for h in range(HEADS):
        here = lane_head == h
        k = jnp.where(here, keys, 0.0).astype(BF16)
        v = jnp.where(here, values, 0.0).astype(BF16)
        s = jnp.where(allowed, dot_nt(q, k) * scale, -jnp.inf)
        e = jnp.exp(s - jnp.max(s, axis=1, keepdims=True))
        p = (e / jnp.sum(e, axis=1, keepdims=True)).astype(BF16)
        part = dot_nn(p, v)
        mixed = part if mixed is None else mixed + part
    return mixed.astype(BF16)


def gelu(x):
    return jax.nn.gelu(x, approximate=True)


def after_attention(x, mixed, gain, w_proj, w_up, w_down):
    x1 = x + dot_nn(mixed, w_proj)
    normed = norm(x1, gain).astype(BF16)
    hidden = gelu(dot_nt(normed, w_up)).astype(BF16)
    return x1 + dot_nn(hidden, w_down)


def token_at(shape, dim):
    t = lax.broadcasted_iota(jnp.int32, shape, dim)
    return t // 64, (t & 7) // 4, t


def half_tokens(x, half):
    to = lax.broadcasted_iota(jnp.int32, (64, 128), 0)
    source = lax.broadcasted_iota(jnp.int32, (64, 128), 1)
    pick = (to // 4) * 8 + half * 4 + (to & 3) == source
    return dot_nn(jnp.where(pick, 1.0, 0.0).astype(BF16), x).astype(BF16)


def block0_kernel(own, own_rows, got, gains, mine, other, state, west, east, qkv_rows, proj_rows):
    n, width = own.shape
    got_top, got_total = top_and_total(got[n:, :n])
    rows = own_rows[...]
    x, _, _ = merged(
        [own[...], got[:n, :].astype(F32)], [rows[0:1], got_top], [rows[1:2], got_total]
    )
    w_qkv, w_proj = attention_weights(0, mine, other, qkv_rows, proj_rows)
    w_up, w_down = mlp_weights(0, mine, other)
    a = norm(x, gains[0:1, :]).astype(BF16)
    qkv = dot_nt(a, w_qkv).astype(BF16).astype(F32)
    allowed = token_at((n, n), 0)[0] == token_at((n, n), 1)[0]
    mixed = attend(
        qkv[:, :width].astype(BF16), qkv[:, width : 2 * width], qkv[:, 2 * width :], allowed
    )
    x = after_attention(x, mixed, gains[1:2, :], w_proj, w_up, w_down)
    state[...] = x
    short = x.astype(BF16)
    west[...] = half_tokens(short, 0)
    east[...] = half_tokens(short, 1)


def block1_kernel(state, from_west, from_east, gains, mine, other, out, qkv_rows, proj_rows):
    n, width = state.shape
    x = state[...]
    w_qkv, w_proj = attention_weights(1, mine, other, qkv_rows, proj_rows)
    w_up, w_down = mlp_weights(1, mine, other)
    sides = jnp.concatenate([from_west[...].astype(F32), from_east[...].astype(F32)], axis=0)
    gain = gains[2:3, :]
    a = norm(x, gain).astype(BF16)
    b = norm(sides, gain).astype(BF16)
    qkv = dot_nt(a, w_qkv).astype(BF16).astype(F32)
    side_kv = dot_nt(b, w_qkv[width:, :]).astype(BF16).astype(F32)
    keys = jnp.concatenate([qkv[:, width : 2 * width], side_kv[:, :width]], axis=0)
    values = jnp.concatenate([qkv[:, 2 * width :], side_kv[:, width:]], axis=0)
    q_block, q_half, _ = token_at((n, 2 * n), 0)
    k_block, k_half, k_at = token_at((n, 2 * n), 1)
    side = k_at - n
    k_block = jnp.where(k_at < n, k_block, (side & 63) // 32)
    k_half = jnp.where(k_at < n, k_half, side // 64)
    allowed = (q_block == k_block) & (q_half == k_half)
    mixed = attend(qkv[:, :width].astype(BF16), keys, values, allowed)
    x = after_attention(x, mixed, gains[3:4, :], w_proj, w_up, w_down)
    final = norm(x, gains[4:5, :]).astype(BF16)
    for j in range(out.shape[0]):
        out[j] = final


def decode_kernel(tokens, weight, out):
    cores, chips, own, width = tokens.shape
    for c in range(2):
        w = weight[c]
        for y in range(chips):
            for core in range(cores):
                at = (y * cores + core) * own
                out[c, at : at + own, :] = dot_nn(tokens[core, y], w).astype(BF16)


def spread_kernel(count, times, *refs):
    parts, outs = refs[:count], refs[-len(times) :]
    height = outs[0].shape[-2]
    at = 0
    for part in parts:
        n = part.shape[0]
        for layer, (out, repeat) in enumerate(zip(outs, times)):
            rows = part[:, layer * height : (layer + 1) * height, :]
            for k in range(repeat):
                out[k, at : at + n] = rows
        at += n


def spread(parts, times, after=()):
    pieces, height, width = parts[0].shape
    total = sum(p.shape[0] for p in parts)
    vmem = pl.BlockSpec(memory_space=pltpu.VMEM)
    return pl.pallas_call(
        functools.partial(spread_kernel, len(parts), times),
        out_shape=[
            jax.ShapeDtypeStruct((n, total, height // len(times), width), BF16) for n in times
        ],
        in_specs=[vmem] * (len(parts) + len(after)),
        out_specs=[vmem] * len(times),
        compiler_params=pltpu.CompilerParams(vmem_limit_bytes=16 * 2**20),
        cost_estimate=pl.CostEstimate(
            flops=0, bytes_accessed=2 * (1 + sum(times)) * total * height * width, transcendentals=0
        ),
    )(*parts, *after)


def copy_kernel(value, *refs):
    for k in range(value.shape[0]):
        refs[-1][k] = value[k]


def held_until(value, after):
    return on_core(copy_kernel, jax.ShapeDtypeStruct(value.shape, value.dtype), moved=2**20)(
        value, *after
    )


def on_core(kernel, outs, scratch=(), flops=0, moved=0, far=()):
    vmem, anywhere = pl.BlockSpec(memory_space=pltpu.VMEM), pl.BlockSpec(memory_space=pl.ANY)

    def call(*operands):
        return pl.pallas_call(
            kernel,
            out_shape=outs,
            in_specs=[anywhere] * len(far) + [vmem] * len(operands),
            out_specs=jax.tree.map(lambda _: vmem, outs),
            scratch_shapes=list(scratch),
            compiler_params=pltpu.CompilerParams(vmem_limit_bytes=40 * 2**20),
            cost_estimate=pl.CostEstimate(flops=flops, bytes_accessed=moved, transcendentals=0),
        )(*far, *operands)

    return call


def shifted(value, axes, size, steps):
    return lax.ppermute(value, axes, [(i, (i + steps) % size) for i in range(size)])


def eastward():
    pairs = []
    for zh in range(2):
        for x in range(4):
            for zl in range(8):
                to = (zh, x, zl + 1) if zl < 7 else (1 - zh, (x + 1) % 4, 0)
                pairs.append(((zh * 4 + x) * 8 + zl, (to[0] * 4 + to[1]) * 8 + to[2]))
    return pairs


def weight_pieces(qkv, proj, up, down):
    core = lax.axis_index("core")
    qkv, up = jnp.swapaxes(qkv, 1, 2), jnp.swapaxes(up, 1, 2)
    attn = jnp.concatenate([qkv, proj], axis=1)
    lanes = [lax.dynamic_slice_in_dim(a, core * 16, 16, 1) for a in (attn, up, down)]
    piece = jnp.concatenate(lanes, axis=1)
    return piece.reshape(1, -1, piece.shape[2])


def body(
    patches,
    embed_weight,
    channel_embed,
    agg_query,
    norm_gains,
    qkv_weight,
    proj_weight,
    up_weight,
    down_weight,
    decode_weight,
):
    chans, rows, cols, width_p = patches.shape
    width = embed_weight.shape[2]
    tokens = rows * cols
    parts = lax.axis_size("y") * lax.axis_size("core")
    own = tokens // parts

    piece = weight_pieces(qkv_weight, proj_weight, up_weight, down_weight)
    (near,) = spread([piece], (8,))
    near = lax.all_to_all(near.reshape(8, -1, width), "zl", 0, 0, tiled=True)

    table = jnp.concatenate(
        [
            embed_weight.reshape(-1, width).astype(F32),
            channel_embed.astype(F32),
            agg_query.reshape(1, width),
            jnp.zeros((8 - chans - 1, width), F32),
        ],
        axis=0,
    )
    message = jax.ShapeDtypeStruct((own + EXTRA, width), BF16)
    messages = jax.ShapeDtypeStruct((4, own + EXTRA, width), BF16)
    stay, leave = on_core(
        embed_kernel,
        (messages, messages),
        [
            pltpu.VMEM((8, tokens), F32),
            pltpu.VMEM((EXTRA, tokens), F32),
        ],
        flops=2 * chans * tokens * width_p * width,
        moved=2 * 2**20,
    )(table, patches.reshape(chans, tokens, width_p))
    got = shifted(leave, "core", 2, 1)
    paired = on_core(pair_kernel, (message,) * 4, moved=2**20)(stay, got)
    along = [shifted(paired[k], "y", 4, k) for k in (1, 2, 3)]
    sent, average, stats = on_core(
        combine_kernel,
        (
            message,
            jax.ShapeDtypeStruct((own, width), F32),
            jax.ShapeDtypeStruct((8, own), F32),
        ),
        flops=6 * 10**10,
    )(paired[0], *along)
    (copies,) = spread([near], (4,), after=(paired[0],))
    mine = lax.all_to_all(copies, "x", 0, 0, tiled=True).reshape(32, -1, width)
    partner = shifted(sent, "zh", 2, 1)
    other = shifted(held_until(mine, (partner,)), "core", 2, 1)

    scratch = [pltpu.VMEM((3 * width, width), F32), pltpu.VMEM((width, width), F32)]
    half = jax.ShapeDtypeStruct((own // 2, width), BF16)
    block_flops = 2 * own * width * width * 12
    state, west, east = on_core(
        block0_kernel,
        (jax.ShapeDtypeStruct((own, width), F32), half, half),
        scratch,
        flops=block_flops,
        moved=4 * 2**20,
    )(average, stats, partner, norm_gains, mine, other)
    pairs = eastward()
    from_west = lax.ppermute(east, ("zh", "x", "zl"), pairs)
    from_east = lax.ppermute(west, ("zh", "x", "zl"), [(b, a) for a, b in pairs])
    final = on_core(
        block1_kernel,
        jax.ShapeDtypeStruct((4, own, width), BF16),
        scratch,
        flops=block_flops,
        moved=4 * 2**20,
    )(state, from_west, from_east, norm_gains, mine, other)
    everyone = lax.all_gather(lax.all_to_all(final, "y", 0, 0, tiled=True), "core")
    decoded = on_core(
        decode_kernel,
        jax.ShapeDtypeStruct((chans, tokens, width_p), BF16),
        flops=2 * chans * tokens * width_p * width,
        moved=2 * 2**20,
    )(everyone, decode_weight)
    return decoded.reshape(chans, rows, cols, width_p)


def solution(mesh):
    fine = Mesh(mesh.devices.reshape(2, 4, 2, 4, 8), ("zh", "y", "core", "x", "zl"))
    chan, lon = ("zh", "y", "core"), ("x", "zl")
    placed = (
        P(chan, None, lon, None),
        P(chan, None, None),
        P(chan, None),
        P(),
        P(),
        P(None, None, lon),
        P(None, lon, None),
        P(None, None, lon),
        P(None, lon, None),
        P(chan, None, None),
    )
    return jax.shard_map(
        body, mesh=fine, in_specs=placed, out_specs=P(chan, None, lon, None), check_vma=False
    )
```

```python
import functools

import jax
import jax.numpy as jnp
from jax import lax
from jax.experimental import pallas as pl
from jax.experimental.pallas import tpu as pltpu
from jax.sharding import Mesh, PartitionSpec as P

HEADS = 8
WC = 8
EPS = 1e-05
F32 = jnp.float32
BF16 = jnp.bfloat16
GROUP = ("y", "core")
EXTRA = 16


def dot_nt(a, b):
    return lax.dot_general(a, b, (((1,), (1,)), ((), ())), preferred_element_type=F32)


def dot_nn(a, b):
    return lax.dot_general(a, b, (((1,), (0,)), ((), ())), preferred_element_type=F32)


def thirds(x):
    hi = x.astype(BF16).astype(F32)
    mid = (x - hi).astype(BF16).astype(F32)
    return hi, mid, (x - hi) - mid


def in_rows(rows, count):
    at = lax.broadcasted_iota(jnp.int32, (count, rows[0].shape[1]), 0)
    out = jnp.zeros((count, rows[0].shape[1]), F32)
    for k, row in enumerate(rows):
        out = jnp.where(at == k, row, out)
    return out


def columns_of(rows):
    n = rows.shape[0]
    full = jnp.concatenate([rows, jnp.zeros((128 - n, 128), F32)], axis=0)
    return full.T


def embed_kernel(table, patches, stay, leave, shares, extras):
    depth = patches.shape[2]
    weight = [table[c * depth : (c + 1) * depth, :].astype(BF16) for c in range(2)]
    chan = table[2 * depth : 2 * depth + 8, :]
    owners = 2 * stay.shape[0]
    own = patches.shape[1] // owners
    q = chan[2:3, :]
    parts = in_rows(thirds(q), 16).astype(BF16)
    scale = q.shape[1] ** (-0.5)
    scores = []
    for c in range(2):
        proj = jnp.sum(dot_nt(parts, weight[c]), axis=0, keepdims=True)
        bias = jnp.sum(chan[c : c + 1, :] * q, axis=1, keepdims=True)
        split = in_rows(thirds(proj), 16).astype(BF16)
        terms = dot_nt(split, patches[c])
        scores.append((jnp.sum(terms, axis=0, keepdims=True) + bias) * scale)
    top = jnp.maximum(scores[0], scores[1])
    first = jnp.exp(scores[0] - top)
    total = first + jnp.exp(scores[1] - top)
    shares[...] = in_rows((first / total,), 8)
    extras[...] = in_rows(thirds(top) + thirds(total), EXTRA)
    chan0, chan1 = chan[0:1, :], chan[1:2, :]
    core = lax.axis_index("core")
    for side, out in enumerate((stay, leave)):
        for y in range(out.shape[0]):
            at = pl.multiple_of((2 * y + (core ^ side)) * own, own)
            e0 = dot_nn(patches[0, pl.ds(at, own), :], weight[0]) + chan0
            e1 = dot_nn(patches[1, pl.ds(at, own), :], weight[1]) + chan1
            w = jnp.broadcast_to(shares[0:1, pl.ds(at, own)], (own, own)).T
            w = jnp.concatenate([w, w], axis=1)
            out[y, :own, :] = (e1 + w * (e0 - e1)).astype(BF16)
            out[y, own:, :own] = extras[:, pl.ds(at, own)].astype(BF16)
            out[y, own:, own:] = jnp.zeros((EXTRA, out.shape[2] - own), BF16)


def top_and_total(block):
    x = block.astype(F32)
    return x[0:1] + (x[1:2] + x[2:3]), x[3:4] + (x[4:5] + x[5:6])


def merged(averages, tops, totals):
    top = functools.reduce(jnp.maximum, tops)
    shares = [t * jnp.exp(m - top) for m, t in zip(tops, totals)]
    total = functools.reduce(jnp.add, shares)
    weights = columns_of(in_rows([s / total for s in shares], 8))
    out = None
    for d, average in enumerate(averages):
        term = weights[:, d : d + 1] * average
        out = term if out is None else out + term
    return out, top, total


def put_message(out, state, top, total):
    n = state.shape[0]
    out[:n, :] = state.astype(BF16)
    out[n:, :n] = in_rows(thirds(top) + thirds(total), EXTRA).astype(BF16)
    out[n:, n:] = jnp.zeros((EXTRA, out.shape[1] - n), BF16)


def merge_messages(messages):
    n = messages[0].shape[0] - EXTRA
    stats = [top_and_total(m[n:, :n]) for m in messages]
    averages = [m[:n, :].astype(F32) for m in messages]
    return merged(averages, [s[0] for s in stats], [s[1] for s in stats])


def pair_kernel(stay, got, *outs):
    y = lax.axis_index("y")
    for k, out in enumerate(outs):
        to = (y + k) & 3
        put_message(out, *merge_messages([stay[to], got[to]]))


def combine_kernel(mine, one, two, three, sent, own, own_rows):
    state, top, total = merge_messages([m[...] for m in (mine, one, two, three)])
    own[...] = state
    own_rows[...] = in_rows([top, total], 8)
    put_message(sent, state, top, total)


def norm(v, gain):
    mean = jnp.mean(v, axis=-1, keepdims=True)
    centred = v - mean
    spread = jnp.mean(centred * centred, axis=-1, keepdims=True)
    return centred * lax.rsqrt(spread + EPS) * gain


def attention_weights(mine, other, qkv_rows, proj_rows):
    first_core = lax.axis_index("core") == 0
    for lon in range(mine.shape[0]):
        a = mine[lon, :16, :].astype(F32)
        b = other[lon, :16, :].astype(F32)
        tail = jnp.where(first_core, b, a)
        qkv_rows[lon * 24 : lon * 24 + 16, :] = jnp.where(first_core, a, b)
        qkv_rows[lon * 24 + 16 : lon * 24 + 24, :] = tail[:8]
        proj_rows[lon * 8 : lon * 8 + 8, :] = tail[8:]
    return qkv_rows[...].astype(BF16), proj_rows[...].astype(BF16)


def mlp_weights(mine, other):
    width = mine.shape[2]

    def rows(at):
        return jnp.concatenate(
            [w[:, at : at + 16, :].reshape(-1, width) for w in (mine, other)], axis=0
        )

    return rows(16), rows(32)


def attend(q, keys, values, allowed):
    width = q.shape[1]
    per_head = width // HEADS
    scale = per_head ** (-0.5)
    lane_head = lax.broadcasted_iota(jnp.int32, keys.shape, 1) // per_head
    mixed = None
    for h in range(HEADS):
        here = lane_head == h
        k = jnp.where(here, keys, 0.0).astype(BF16)
        v = jnp.where(here, values, 0.0).astype(BF16)
        s = jnp.where(allowed, dot_nt(q, k) * scale, -jnp.inf)
        e = jnp.exp(s - jnp.max(s, axis=1, keepdims=True))
        p = (e / jnp.sum(e, axis=1, keepdims=True)).astype(BF16)
        part = dot_nn(p, v)
        mixed = part if mixed is None else mixed + part
    return mixed.astype(BF16)


def gelu(x):
    return jax.nn.gelu(x, approximate=True)


def after_attention(x, mixed, gain, w_proj, w_up, w_down):
    x1 = x + dot_nn(mixed, w_proj)
    normed = norm(x1, gain).astype(BF16)
    hidden = gelu(dot_nt(normed, w_up)).astype(BF16)
    return x1 + dot_nn(hidden, w_down)


def token_at(shape, dim):
    t = lax.broadcasted_iota(jnp.int32, shape, dim)
    return t // 64, (t & 7) // 4, t


def half_tokens(x, half):
    to = lax.broadcasted_iota(jnp.int32, (64, 128), 0)
    source = lax.broadcasted_iota(jnp.int32, (64, 128), 1)
    pick = (to // 4) * 8 + half * 4 + (to & 3) == source
    return dot_nn(jnp.where(pick, 1.0, 0.0).astype(BF16), x).astype(BF16)


def whole_kernel(own, own_rows, got, state):
    n = own.shape[0]
    got_top, got_total = top_and_total(got[n:, :n])
    rows = own_rows[...]
    state[...], _, _ = merged(
        [own[...], got[:n, :].astype(F32)], [rows[0:1], got_top], [rows[1:2], got_total]
    )


def block0_kernel(start, gains, mine, other, state, near, far, qkv_rows, proj_rows):
    n, width = start.shape
    x = start[...]
    w_qkv, w_proj = attention_weights(mine, other, qkv_rows, proj_rows)
    w_up, w_down = mlp_weights(mine, other)
    a = norm(x, gains[0:1, :]).astype(BF16)
    qkv = dot_nt(a, w_qkv).astype(BF16).astype(F32)
    allowed = token_at((n, n), 0)[0] == token_at((n, n), 1)[0]
    mixed = attend(
        qkv[:, :width].astype(BF16), qkv[:, width : 2 * width], qkv[:, 2 * width :], allowed
    )
    x = after_attention(x, mixed, gains[1:2, :], w_proj, w_up, w_down)
    state[...] = x
    short = x.astype(BF16)
    odd = lax.axis_index("zl") & 1
    near[...] = half_tokens(short, 1 - odd)
    far[...] = half_tokens(short, odd)


def sides_kernel(from_near, from_far, gains, out):
    odd = (lax.axis_index("zl") & 1) == 1
    near, far = from_near[...].astype(F32), from_far[...].astype(F32)
    sides = jnp.concatenate([jnp.where(odd, near, far), jnp.where(odd, far, near)], axis=0)
    out[...] = norm(sides, gains[2:3, :]).astype(BF16)


def block1_kernel(state, sides, gains, mine, other, out, qkv_rows, proj_rows):
    n, width = state.shape
    x = state[...]
    w_qkv, w_proj = attention_weights(mine, other, qkv_rows, proj_rows)
    w_up, w_down = mlp_weights(mine, other)
    a = norm(x, gains[2:3, :]).astype(BF16)
    qkv = dot_nt(a, w_qkv).astype(BF16).astype(F32)
    side_kv = dot_nt(sides[...], w_qkv[width:, :]).astype(BF16).astype(F32)
    keys = jnp.concatenate([qkv[:, width : 2 * width], side_kv[:, :width]], axis=0)
    values = jnp.concatenate([qkv[:, 2 * width :], side_kv[:, width:]], axis=0)
    q_block, q_half, _ = token_at((n, 2 * n), 0)
    k_block, k_half, k_at = token_at((n, 2 * n), 1)
    side = k_at - n
    k_block = jnp.where(k_at < n, k_block, (side & 63) // 32)
    k_half = jnp.where(k_at < n, k_half, side // 64)
    allowed = (q_block == k_block) & (q_half == k_half)
    mixed = attend(qkv[:, :width].astype(BF16), keys, values, allowed)
    x = after_attention(x, mixed, gains[3:4, :], w_proj, w_up, w_down)
    final = norm(x, gains[4:5, :]).astype(BF16)
    for j in range(out.shape[0]):
        out[j] = final


def decode_kernel(tokens, weight, out):
    cores, chips, own, width = tokens.shape
    for c in range(2):
        w = weight[c]
        for y in range(chips):
            for core in range(cores):
                at = (y * cores + core) * own
                out[c, at : at + own, :] = dot_nn(tokens[core, y], w).astype(BF16)


def spread_kernel(count, times, *refs):
    parts, outs = refs[:count], refs[-len(times) :]
    height = outs[0].shape[-2]
    at = 0
    for part in parts:
        n = part.shape[0]
        for layer, (out, repeat) in enumerate(zip(outs, times)):
            rows = part[:, layer * height : (layer + 1) * height, :]
            for k in range(repeat):
                out[k, at : at + n] = rows
        at += n


def spread(parts, times, after=()):
    pieces, height, width = parts[0].shape
    total = sum(p.shape[0] for p in parts)
    vmem = pl.BlockSpec(memory_space=pltpu.VMEM)
    return pl.pallas_call(
        functools.partial(spread_kernel, len(parts), times),
        out_shape=[
            jax.ShapeDtypeStruct((n, total, height // len(times), width), BF16) for n in times
        ],
        in_specs=[vmem] * (len(parts) + len(after)),
        out_specs=[vmem] * len(times),
        compiler_params=pltpu.CompilerParams(vmem_limit_bytes=16 * 2**20),
        cost_estimate=pl.CostEstimate(
            flops=0, bytes_accessed=2 * (1 + sum(times)) * total * height * width, transcendentals=0
        ),
    )(*parts, *after)


def copy_kernel(value, *refs):
    for k in range(value.shape[0]):
        refs[-1][k] = value[k]


def held_until(value, after):
    return on_core(copy_kernel, jax.ShapeDtypeStruct(value.shape, value.dtype), moved=2**20)(
        value, *after
    )


def on_core(kernel, outs, scratch=(), flops=0, moved=0, far=()):
    vmem, anywhere = pl.BlockSpec(memory_space=pltpu.VMEM), pl.BlockSpec(memory_space=pl.ANY)

    def call(*operands):
        return pl.pallas_call(
            kernel,
            out_shape=outs,
            in_specs=[anywhere] * len(far) + [vmem] * len(operands),
            out_specs=jax.tree.map(lambda _: vmem, outs),
            scratch_shapes=list(scratch),
            compiler_params=pltpu.CompilerParams(vmem_limit_bytes=40 * 2**20),
            cost_estimate=pl.CostEstimate(flops=flops, bytes_accessed=moved, transcendentals=0),
        )(*far, *operands)

    return call


def shifted(value, axes, size, steps):
    return lax.ppermute(value, axes, [(i, (i + steps) % size) for i in range(size)])


def swaps():
    def at(zh, x, zl):
        return (zh * 4 + x) * 8 + zl

    near, far = [], []
    for zh in range(2):
        for x in range(4):
            near += [(at(zh, x, zl), at(zh, x, zl ^ 1)) for zl in range(8)]
            far += [(at(zh, x, zl), at(zh, x, zl + 1)) for zl in (1, 3, 5)]
            far += [(at(zh, x, zl), at(zh, x, zl - 1)) for zl in (2, 4, 6)]
            far.append((at(zh, x, 7), at(1 - zh, (x + 1) % 4, 0)))
            far.append((at(zh, x, 0), at(1 - zh, (x + 3) % 4, 7)))
    return near, far


def weight_pieces(qkv, proj, up, down):
    core = lax.axis_index("core")
    qkv, up = jnp.swapaxes(qkv, 1, 2), jnp.swapaxes(up, 1, 2)
    attn = jnp.concatenate([qkv, proj], axis=1)
    lanes = [lax.dynamic_slice_in_dim(a, core * 16, 16, 1) for a in (attn, up, down)]
    piece = jnp.concatenate(lanes, axis=1)
    return piece.reshape(1, -1, piece.shape[2])


def body(
    patches,
    embed_weight,
    channel_embed,
    agg_query,
    norm_gains,
    qkv_weight,
    proj_weight,
    up_weight,
    down_weight,
    decode_weight,
):
    chans, rows, cols, width_p = patches.shape
    width = embed_weight.shape[2]
    tokens = rows * cols
    parts = lax.axis_size("y") * lax.axis_size("core")
    own = tokens // parts

    piece = weight_pieces(qkv_weight, proj_weight, up_weight, down_weight)
    (near,) = spread([piece], (8,))
    near = lax.all_to_all(near.reshape(8, -1, width), "zl", 0, 0, tiled=True)

    table = jnp.concatenate(
        [
            embed_weight.reshape(-1, width).astype(F32),
            channel_embed.astype(F32),
            agg_query.reshape(1, width),
            jnp.zeros((8 - chans - 1, width), F32),
        ],
        axis=0,
    )
    message = jax.ShapeDtypeStruct((own + EXTRA, width), BF16)
    messages = jax.ShapeDtypeStruct((4, own + EXTRA, width), BF16)
    stay, leave = on_core(
        embed_kernel,
        (messages, messages),
        [
            pltpu.VMEM((8, tokens), F32),
            pltpu.VMEM((EXTRA, tokens), F32),
        ],
        flops=2 * chans * tokens * width_p * width,
        moved=2 * 2**20,
    )(table, patches.reshape(chans, tokens, width_p))
    got = shifted(leave, "core", 2, 1)
    paired = on_core(pair_kernel, (message,) * 4, moved=2**20)(stay, got)
    along = [shifted(paired[k], "y", 4, k) for k in (1, 2, 3)]
    sent, average, stats = on_core(
        combine_kernel,
        (
            message,
            jax.ShapeDtypeStruct((own, width), F32),
            jax.ShapeDtypeStruct((8, own), F32),
        ),
        flops=6 * 10**10,
    )(paired[0], *along)
    copies0, copies1 = spread([near], (4, 4), after=(paired[0],))
    mine0 = lax.all_to_all(copies0, "x", 0, 0, tiled=True).reshape(32, -1, width)
    mine1 = lax.all_to_all(copies1, "x", 0, 0, tiled=True).reshape(32, -1, width)
    partner = shifted(sent, "zh", 2, 1)
    other0 = shifted(mine0, "core", 2, 1)
    start = on_core(
        whole_kernel, jax.ShapeDtypeStruct((own, width), F32), flops=6 * 10**10
    )(average, stats, partner)

    scratch = [pltpu.VMEM((3 * width, width), F32), pltpu.VMEM((width, width), F32)]
    half = jax.ShapeDtypeStruct((own // 2, width), BF16)
    block_flops = 2 * own * width * width * 12
    state, to_near, to_far = on_core(
        block0_kernel,
        (jax.ShapeDtypeStruct((own, width), F32), half, half),
        scratch,
        flops=block_flops,
        moved=4 * 2**20,
    )(start, norm_gains, mine0, other0)
    near_pairs, far_pairs = swaps()
    from_near = lax.ppermute(to_near, ("zh", "x", "zl"), near_pairs)
    from_far = lax.ppermute(to_far, ("zh", "x", "zl"), far_pairs)
    other1 = shifted(held_until(mine1, (to_far,)), "core", 2, 1)
    sides = on_core(
        sides_kernel, jax.ShapeDtypeStruct((own, width), BF16), flops=6 * 10**10
    )(from_near, from_far, norm_gains)
    final = on_core(
        block1_kernel,
        jax.ShapeDtypeStruct((4, own, width), BF16),
        scratch,
        flops=block_flops,
        moved=4 * 2**20,
    )(state, sides, norm_gains, mine1, other1)
    everyone = lax.all_gather(lax.all_to_all(final, "y", 0, 0, tiled=True), "core")
    decoded = on_core(
        decode_kernel,
        jax.ShapeDtypeStruct((chans, tokens, width_p), BF16),
        flops=2 * chans * tokens * width_p * width,
        moved=2 * 2**20,
    )(everyone, decode_weight)
    return decoded.reshape(chans, rows, cols, width_p)


def solution(mesh):
    fine = Mesh(mesh.devices.reshape(2, 4, 2, 4, 8), ("zh", "y", "core", "x", "zl"))
    chan, lon = ("zh", "y", "core"), ("x", "zl")
    placed = (
        P(chan, None, lon, None),
        P(chan, None, None),
        P(chan, None),
        P(),
        P(),
        P(None, None, lon),
        P(None, lon, None),
        P(None, None, lon),
        P(None, lon, None),
        P(chan, None, None),
    )
    return jax.shard_map(
        body, mesh=fine, in_specs=placed, out_specs=P(chan, None, lon, None), check_vma=False
    )
```

```python
import functools

import jax
import jax.numpy as jnp
from jax import lax
from jax.experimental import pallas as pl
from jax.experimental.pallas import tpu as pltpu
from jax.sharding import Mesh, PartitionSpec as P

HEADS = 8
WC = 8
EPS = 1e-05
F32 = jnp.float32
BF16 = jnp.bfloat16
GROUP = ("y", "core")
EXTRA = 16


def dot_nt(a, b):
    return lax.dot_general(a, b, (((1,), (1,)), ((), ())), preferred_element_type=F32)


def dot_nn(a, b):
    return lax.dot_general(a, b, (((1,), (0,)), ((), ())), preferred_element_type=F32)


def thirds(x):
    hi = x.astype(BF16).astype(F32)
    mid = (x - hi).astype(BF16).astype(F32)
    return hi, mid, (x - hi) - mid


def in_rows(rows, count):
    at = lax.broadcasted_iota(jnp.int32, (count, rows[0].shape[1]), 0)
    out = jnp.zeros((count, rows[0].shape[1]), F32)
    for k, row in enumerate(rows):
        out = jnp.where(at == k, row, out)
    return out


def columns_of(rows):
    n = rows.shape[0]
    full = jnp.concatenate([rows, jnp.zeros((128 - n, 128), F32)], axis=0)
    return full.T


def embed_kernel(table, patches, stay, leave, shares, extras):
    depth = patches.shape[2]
    weight = [table[c * depth : (c + 1) * depth, :].astype(BF16) for c in range(2)]
    chan = table[2 * depth : 2 * depth + 8, :]
    owners = 2 * stay.shape[0]
    own = patches.shape[1] // owners
    q = chan[2:3, :]
    parts = in_rows(thirds(q), 16).astype(BF16)
    scale = q.shape[1] ** (-0.5)
    scores = []
    for c in range(2):
        proj = jnp.sum(dot_nt(parts, weight[c]), axis=0, keepdims=True)
        bias = jnp.sum(chan[c : c + 1, :] * q, axis=1, keepdims=True)
        split = in_rows(thirds(proj), 16).astype(BF16)
        terms = dot_nt(split, patches[c])
        scores.append((jnp.sum(terms, axis=0, keepdims=True) + bias) * scale)
    top = jnp.maximum(scores[0], scores[1])
    first = jnp.exp(scores[0] - top)
    total = first + jnp.exp(scores[1] - top)
    shares[...] = in_rows((first / total,), 8)
    extras[...] = in_rows(thirds(top) + thirds(total), EXTRA)
    chan0, chan1 = chan[0:1, :], chan[1:2, :]
    core = lax.axis_index("core")
    for side, out in enumerate((stay, leave)):
        for y in range(out.shape[0]):
            at = pl.multiple_of((2 * y + (core ^ side)) * own, own)
            e0 = dot_nn(patches[0, pl.ds(at, own), :], weight[0]) + chan0
            e1 = dot_nn(patches[1, pl.ds(at, own), :], weight[1]) + chan1
            w = jnp.broadcast_to(shares[0:1, pl.ds(at, own)], (own, own)).T
            w = jnp.concatenate([w, w], axis=1)
            out[y, :own, :] = (e1 + w * (e0 - e1)).astype(BF16)
            out[y, own:, :own] = extras[:, pl.ds(at, own)].astype(BF16)
            out[y, own:, own:] = jnp.zeros((EXTRA, out.shape[2] - own), BF16)


def top_and_total(block):
    x = block.astype(F32)
    return x[0:1] + (x[1:2] + x[2:3]), x[3:4] + (x[4:5] + x[5:6])


def merged(averages, tops, totals):
    top = functools.reduce(jnp.maximum, tops)
    shares = [t * jnp.exp(m - top) for m, t in zip(tops, totals)]
    total = functools.reduce(jnp.add, shares)
    weights = columns_of(in_rows([s / total for s in shares], 8))
    out = None
    for d, average in enumerate(averages):
        term = weights[:, d : d + 1] * average
        out = term if out is None else out + term
    return out, top, total


def put_message(out, state, top, total):
    n = state.shape[0]
    out[:n, :] = state.astype(BF16)
    out[n:, :n] = in_rows(thirds(top) + thirds(total), EXTRA).astype(BF16)
    out[n:, n:] = jnp.zeros((EXTRA, out.shape[1] - n), BF16)


def merge_messages(messages):
    n = messages[0].shape[0] - EXTRA
    stats = [top_and_total(m[n:, :n]) for m in messages]
    averages = [m[:n, :].astype(F32) for m in messages]
    return merged(averages, [s[0] for s in stats], [s[1] for s in stats])


def pair_kernel(stay, got, *outs):
    y = lax.axis_index("y")
    for k, out in enumerate(outs):
        to = (y + k) & 3
        put_message(out, *merge_messages([stay[to], got[to]]))


def combine_kernel(mine, one, two, three, sent, own, own_rows):
    state, top, total = merge_messages([m[...] for m in (mine, one, two, three)])
    own[...] = state
    own_rows[...] = in_rows([top, total], 8)
    put_message(sent, state, top, total)


def norm(v, gain):
    mean = jnp.mean(v, axis=-1, keepdims=True)
    centred = v - mean
    spread = jnp.mean(centred * centred, axis=-1, keepdims=True)
    return centred * lax.rsqrt(spread + EPS) * gain


def attention_weights(mine, other, qkv_rows, proj_rows):
    first_core = lax.axis_index("core") == 0
    for lon in range(mine.shape[0]):
        a = mine[lon, :16, :].astype(F32)
        b = other[lon, :16, :].astype(F32)
        tail = jnp.where(first_core, b, a)
        qkv_rows[lon * 24 : lon * 24 + 16, :] = jnp.where(first_core, a, b)
        qkv_rows[lon * 24 + 16 : lon * 24 + 24, :] = tail[:8]
        proj_rows[lon * 8 : lon * 8 + 8, :] = tail[8:]
    return qkv_rows[...].astype(BF16), proj_rows[...].astype(BF16)


def mlp_weights(mine, other):
    width = mine.shape[2]

    def rows(at):
        return jnp.concatenate(
            [w[:, at : at + 16, :].reshape(-1, width) for w in (mine, other)], axis=0
        )

    return rows(16), rows(32)


def attend(q, keys, values, allowed):
    width = q.shape[1]
    per_head = width // HEADS
    scale = per_head ** (-0.5)
    lane_head = lax.broadcasted_iota(jnp.int32, keys.shape, 1) // per_head
    mixed = None
    for h in range(HEADS):
        here = lane_head == h
        k = jnp.where(here, keys, 0.0).astype(BF16)
        v = jnp.where(here, values, 0.0).astype(BF16)
        s = jnp.where(allowed, dot_nt(q, k) * scale, -jnp.inf)
        e = jnp.exp(s - jnp.max(s, axis=1, keepdims=True))
        p = (e / jnp.sum(e, axis=1, keepdims=True)).astype(BF16)
        part = dot_nn(p, v)
        mixed = part if mixed is None else mixed + part
    return mixed.astype(BF16)


def gelu(x):
    return jax.nn.gelu(x, approximate=True)


def after_attention(x, mixed, gain, w_proj, w_up, w_down):
    x1 = x + dot_nn(mixed, w_proj)
    normed = norm(x1, gain).astype(BF16)
    hidden = gelu(dot_nt(normed, w_up)).astype(BF16)
    return x1 + dot_nn(hidden, w_down)


def token_at(shape, dim):
    t = lax.broadcasted_iota(jnp.int32, shape, dim)
    return t // 64, (t & 7) // 4, t


def half_tokens(x, half):
    to = lax.broadcasted_iota(jnp.int32, (64, 128), 0)
    source = lax.broadcasted_iota(jnp.int32, (64, 128), 1)
    pick = (to // 4) * 8 + half * 4 + (to & 3) == source
    return dot_nn(jnp.where(pick, 1.0, 0.0).astype(BF16), x).astype(BF16)


def whole_kernel(own, own_rows, got, state):
    n = own.shape[0]
    got_top, got_total = top_and_total(got[n:, :n])
    rows = own_rows[...]
    state[...], _, _ = merged(
        [own[...], got[:n, :].astype(F32)], [rows[0:1], got_top], [rows[1:2], got_total]
    )


def block0_kernel(start, gains, mine, other, state, far, near, qkv_rows, proj_rows):
    n, width = start.shape
    x = start[...]
    w_qkv, w_proj = attention_weights(mine, other, qkv_rows, proj_rows)
    w_up, w_down = mlp_weights(mine, other)
    a = norm(x, gains[0:1, :]).astype(BF16)
    qkv = dot_nt(a, w_qkv).astype(BF16).astype(F32)
    allowed = token_at((n, n), 0)[0] == token_at((n, n), 1)[0]
    mixed = attend(
        qkv[:, :width].astype(BF16), qkv[:, width : 2 * width], qkv[:, 2 * width :], allowed
    )
    x = after_attention(x, mixed, gains[1:2, :], w_proj, w_up, w_down)
    state[...] = x
    short = x.astype(BF16)
    odd = lax.axis_index("zl") & 1
    near[...] = half_tokens(short, 1 - odd)
    far[...] = half_tokens(short, odd)


def sides_kernel(from_far, from_near, gains, out):
    odd = (lax.axis_index("zl") & 1) == 1
    near, far = from_near[...].astype(F32), from_far[...].astype(F32)
    sides = jnp.concatenate([jnp.where(odd, near, far), jnp.where(odd, far, near)], axis=0)
    out[...] = norm(sides, gains[2:3, :]).astype(BF16)


def block1_kernel(state, sides, gains, mine, other, out, qkv_rows, proj_rows):
    n, width = state.shape
    x = state[...]
    w_qkv, w_proj = attention_weights(mine, other, qkv_rows, proj_rows)
    w_up, w_down = mlp_weights(mine, other)
    a = norm(x, gains[2:3, :]).astype(BF16)
    qkv = dot_nt(a, w_qkv).astype(BF16).astype(F32)
    side_kv = dot_nt(sides[...], w_qkv[width:, :]).astype(BF16).astype(F32)
    keys = jnp.concatenate([qkv[:, width : 2 * width], side_kv[:, :width]], axis=0)
    values = jnp.concatenate([qkv[:, 2 * width :], side_kv[:, width:]], axis=0)
    q_block, q_half, _ = token_at((n, 2 * n), 0)
    k_block, k_half, k_at = token_at((n, 2 * n), 1)
    side = k_at - n
    k_block = jnp.where(k_at < n, k_block, (side & 63) // 32)
    k_half = jnp.where(k_at < n, k_half, side // 64)
    allowed = (q_block == k_block) & (q_half == k_half)
    mixed = attend(qkv[:, :width].astype(BF16), keys, values, allowed)
    x = after_attention(x, mixed, gains[3:4, :], w_proj, w_up, w_down)
    final = norm(x, gains[4:5, :]).astype(BF16)
    for j in range(out.shape[0]):
        out[j] = final


def decode_kernel(tokens, weight, out):
    cores, chips, own, width = tokens.shape
    for c in range(2):
        w = weight[c]
        for y in range(chips):
            for core in range(cores):
                at = (y * cores + core) * own
                out[c, at : at + own, :] = dot_nn(tokens[core, y], w).astype(BF16)


def spread_kernel(count, times, *refs):
    parts, outs = refs[:count], refs[-len(times) :]
    height = outs[0].shape[-2]
    at = 0
    for part in parts:
        n = part.shape[0]
        for layer, (out, repeat) in enumerate(zip(outs, times)):
            rows = part[:, layer * height : (layer + 1) * height, :]
            for k in range(repeat):
                out[k, at : at + n] = rows
        at += n


def spread(parts, times, after=(), flops=0):
    pieces, height, width = parts[0].shape
    total = sum(p.shape[0] for p in parts)
    vmem = pl.BlockSpec(memory_space=pltpu.VMEM)
    return pl.pallas_call(
        functools.partial(spread_kernel, len(parts), times),
        out_shape=[
            jax.ShapeDtypeStruct((n, total, height // len(times), width), BF16) for n in times
        ],
        in_specs=[vmem] * (len(parts) + len(after)),
        out_specs=[vmem] * len(times),
        compiler_params=pltpu.CompilerParams(vmem_limit_bytes=16 * 2**20),
        cost_estimate=pl.CostEstimate(
            flops=flops, bytes_accessed=2 * (1 + sum(times)) * total * height * width, transcendentals=0
        ),
    )(*parts, *after)


def copy_kernel(value, *refs):
    for k in range(value.shape[0]):
        refs[-1][k] = value[k]


def held_until(value, after):
    return on_core(copy_kernel, jax.ShapeDtypeStruct(value.shape, value.dtype), moved=2**20)(
        value, *after
    )


def on_core(kernel, outs, scratch=(), flops=0, moved=0, far=()):
    vmem, anywhere = pl.BlockSpec(memory_space=pltpu.VMEM), pl.BlockSpec(memory_space=pl.ANY)

    def call(*operands):
        return pl.pallas_call(
            kernel,
            out_shape=outs,
            in_specs=[anywhere] * len(far) + [vmem] * len(operands),
            out_specs=jax.tree.map(lambda _: vmem, outs),
            scratch_shapes=list(scratch),
            compiler_params=pltpu.CompilerParams(vmem_limit_bytes=40 * 2**20),
            cost_estimate=pl.CostEstimate(flops=flops, bytes_accessed=moved, transcendentals=0),
        )(*far, *operands)

    return call


def shifted(value, axes, size, steps):
    return lax.ppermute(value, axes, [(i, (i + steps) % size) for i in range(size)])


def swaps():
    def at(zh, x, zl):
        return (zh * 4 + x) * 8 + zl

    near, far = [], []
    for zh in range(2):
        for x in range(4):
            near += [(at(zh, x, zl), at(zh, x, zl ^ 1)) for zl in range(8)]
            far += [(at(zh, x, zl), at(zh, x, zl + 1)) for zl in (1, 3, 5)]
            far += [(at(zh, x, zl), at(zh, x, zl - 1)) for zl in (2, 4, 6)]
            far.append((at(zh, x, 7), at(1 - zh, (x + 1) % 4, 0)))
            far.append((at(zh, x, 0), at(1 - zh, (x + 3) % 4, 7)))
    return near, far


def weight_pieces(qkv, proj, up, down):
    core = lax.axis_index("core")
    qkv, up = jnp.swapaxes(qkv, 1, 2), jnp.swapaxes(up, 1, 2)
    attn = jnp.concatenate([qkv, proj], axis=1)
    lanes = [lax.dynamic_slice_in_dim(a, core * 16, 16, 1) for a in (attn, up, down)]
    piece = jnp.concatenate(lanes, axis=1)
    return piece.reshape(1, -1, piece.shape[2])


def body(
    patches,
    embed_weight,
    channel_embed,
    agg_query,
    norm_gains,
    qkv_weight,
    proj_weight,
    up_weight,
    down_weight,
    decode_weight,
):
    chans, rows, cols, width_p = patches.shape
    width = embed_weight.shape[2]
    tokens = rows * cols
    parts = lax.axis_size("y") * lax.axis_size("core")
    own = tokens // parts

    piece = weight_pieces(qkv_weight, proj_weight, up_weight, down_weight)
    (near,) = spread([piece], (8,))
    near = lax.all_to_all(near.reshape(8, -1, width), "zl", 0, 0, tiled=True)

    table = jnp.concatenate(
        [
            embed_weight.reshape(-1, width).astype(F32),
            channel_embed.astype(F32),
            agg_query.reshape(1, width),
            jnp.zeros((8 - chans - 1, width), F32),
        ],
        axis=0,
    )
    message = jax.ShapeDtypeStruct((own + EXTRA, width), BF16)
    messages = jax.ShapeDtypeStruct((4, own + EXTRA, width), BF16)
    stay, leave = on_core(
        embed_kernel,
        (messages, messages),
        [
            pltpu.VMEM((8, tokens), F32),
            pltpu.VMEM((EXTRA, tokens), F32),
        ],
        flops=2 * chans * tokens * width_p * width,
        moved=2 * 2**20,
    )(table, patches.reshape(chans, tokens, width_p))
    got = shifted(leave, "core", 2, 1)
    paired = on_core(pair_kernel, (message,) * 4, moved=2**20)(stay, got)
    along = [shifted(paired[k], "y", 4, k) for k in (1, 2, 3)]
    sent, average, stats = on_core(
        combine_kernel,
        (
            message,
            jax.ShapeDtypeStruct((own, width), F32),
            jax.ShapeDtypeStruct((8, own), F32),
        ),
        flops=6 * 10**10,
    )(paired[0], *along)
    copies0, near1 = spread([near], (4, 1), after=(paired[0],))
    mine0 = lax.all_to_all(copies0, "x", 0, 0, tiled=True).reshape(32, -1, width)
    (copies1,) = spread([near1[0]], (4,), after=(mine0,), flops=0)
    mine1 = lax.all_to_all(copies1, "x", 0, 0, tiled=True).reshape(32, -1, width)
    partner = shifted(sent, "zh", 2, 1)
    other0 = shifted(mine0, "core", 2, 1)
    start = on_core(
        whole_kernel, jax.ShapeDtypeStruct((own, width), F32), flops=6 * 10**10
    )(average, stats, partner)

    scratch = [pltpu.VMEM((3 * width, width), F32), pltpu.VMEM((width, width), F32)]
    half = jax.ShapeDtypeStruct((own // 2, width), BF16)
    block_flops = 2 * own * width * width * 12
    state, to_far, to_near = on_core(
        block0_kernel,
        (jax.ShapeDtypeStruct((own, width), F32), half, half),
        scratch,
        flops=block_flops,
        moved=4 * 2**20,
    )(start, norm_gains, mine0, other0)
    near_pairs, far_pairs = swaps()
    from_far = lax.ppermute(to_far, ("zh", "x", "zl"), far_pairs)
    from_near = lax.ppermute(to_near, ("zh", "x", "zl"), near_pairs)
    other1 = shifted(held_until(mine1, (to_near,)), "core", 2, 1)
    sides = on_core(
        sides_kernel, jax.ShapeDtypeStruct((own, width), BF16), flops=6 * 10**10
    )(from_far, from_near, norm_gains)
    final = on_core(
        block1_kernel,
        jax.ShapeDtypeStruct((4, own, width), BF16),
        scratch,
        flops=block_flops,
        moved=4 * 2**20,
    )(state, sides, norm_gains, mine1, other1)
    everyone = lax.all_gather(lax.all_to_all(final, "y", 0, 0, tiled=True), "core")
    decoded = on_core(
        decode_kernel,
        jax.ShapeDtypeStruct((chans, tokens, width_p), BF16),
        flops=2 * chans * tokens * width_p * width,
        moved=2 * 2**20,
    )(everyone, decode_weight)
    return decoded.reshape(chans, rows, cols, width_p)


def solution(mesh):
    fine = Mesh(mesh.devices.reshape(2, 4, 2, 4, 8), ("zh", "y", "core", "x", "zl"))
    chan, lon = ("zh", "y", "core"), ("x", "zl")
    placed = (
        P(chan, None, lon, None),
        P(chan, None, None),
        P(chan, None),
        P(),
        P(),
        P(None, None, lon),
        P(None, lon, None),
        P(None, None, lon),
        P(None, lon, None),
        P(chan, None, None),
    )
    return jax.shard_map(
        body, mesh=fine, in_specs=placed, out_specs=P(chan, None, lon, None), check_vma=False
    )
```

```python
import functools

import jax
import jax.numpy as jnp
from jax import lax
from jax.experimental import pallas as pl
from jax.experimental.pallas import tpu as pltpu
from jax.sharding import Mesh, PartitionSpec as P

HEADS = 8
WC = 8
EPS = 1e-05
F32 = jnp.float32
BF16 = jnp.bfloat16
GROUP = ("y", "core")
EXTRA = 16


def dot_nt(a, b):
    return lax.dot_general(a, b, (((1,), (1,)), ((), ())), preferred_element_type=F32)


def dot_nn(a, b):
    return lax.dot_general(a, b, (((1,), (0,)), ((), ())), preferred_element_type=F32)


def thirds(x):
    hi = x.astype(BF16).astype(F32)
    mid = (x - hi).astype(BF16).astype(F32)
    return hi, mid, (x - hi) - mid


def in_rows(rows, count):
    at = lax.broadcasted_iota(jnp.int32, (count, rows[0].shape[1]), 0)
    out = jnp.zeros((count, rows[0].shape[1]), F32)
    for k, row in enumerate(rows):
        out = jnp.where(at == k, row, out)
    return out


def columns_of(rows):
    n = rows.shape[0]
    full = jnp.concatenate([rows, jnp.zeros((128 - n, 128), F32)], axis=0)
    return full.T


def embed_kernel(table, patches, stay, leave, shares, extras):
    depth = patches.shape[2]
    weight = [table[c * depth : (c + 1) * depth, :].astype(BF16) for c in range(2)]
    chan = table[2 * depth : 2 * depth + 8, :]
    owners = 2 * stay.shape[0]
    own = patches.shape[1] // owners
    q = chan[2:3, :]
    parts = in_rows(thirds(q), 16).astype(BF16)
    scale = q.shape[1] ** (-0.5)
    scores = []
    for c in range(2):
        proj = jnp.sum(dot_nt(parts, weight[c]), axis=0, keepdims=True)
        bias = jnp.sum(chan[c : c + 1, :] * q, axis=1, keepdims=True)
        split = in_rows(thirds(proj), 16).astype(BF16)
        terms = dot_nt(split, patches[c])
        scores.append((jnp.sum(terms, axis=0, keepdims=True) + bias) * scale)
    top = jnp.maximum(scores[0], scores[1])
    first = jnp.exp(scores[0] - top)
    total = first + jnp.exp(scores[1] - top)
    shares[...] = in_rows((first / total,), 8)
    extras[...] = in_rows(thirds(top) + thirds(total), EXTRA)
    chan0, chan1 = chan[0:1, :], chan[1:2, :]
    core = lax.axis_index("core")
    for side, out in enumerate((stay, leave)):
        for y in range(out.shape[0]):
            at = pl.multiple_of((2 * y + (core ^ side)) * own, own)
            e0 = dot_nn(patches[0, pl.ds(at, own), :], weight[0]) + chan0
            e1 = dot_nn(patches[1, pl.ds(at, own), :], weight[1]) + chan1
            w = jnp.broadcast_to(shares[0:1, pl.ds(at, own)], (own, own)).T
            w = jnp.concatenate([w, w], axis=1)
            out[y, :own, :] = (e1 + w * (e0 - e1)).astype(BF16)
            out[y, own:, :own] = extras[:, pl.ds(at, own)].astype(BF16)
            out[y, own:, own:] = jnp.zeros((EXTRA, out.shape[2] - own), BF16)


def top_and_total(block):
    x = block.astype(F32)
    return x[0:1] + (x[1:2] + x[2:3]), x[3:4] + (x[4:5] + x[5:6])


def merged(averages, tops, totals):
    top = functools.reduce(jnp.maximum, tops)
    shares = [t * jnp.exp(m - top) for m, t in zip(tops, totals)]
    total = functools.reduce(jnp.add, shares)
    weights = columns_of(in_rows([s / total for s in shares], 8))
    out = None
    for d, average in enumerate(averages):
        term = weights[:, d : d + 1] * average
        out = term if out is None else out + term
    return out, top, total


def put_message(out, state, top, total):
    n = state.shape[0]
    out[:n, :] = state.astype(BF16)
    out[n:, :n] = in_rows(thirds(top) + thirds(total), EXTRA).astype(BF16)
    out[n:, n:] = jnp.zeros((EXTRA, out.shape[1] - n), BF16)


def merge_messages(messages):
    n = messages[0].shape[0] - EXTRA
    stats = [top_and_total(m[n:, :n]) for m in messages]
    averages = [m[:n, :].astype(F32) for m in messages]
    return merged(averages, [s[0] for s in stats], [s[1] for s in stats])


def pair_kernel(stay, got, *outs):
    y = lax.axis_index("y")
    for k, out in enumerate(outs):
        to = (y + k) & 3
        put_message(out, *merge_messages([stay[to], got[to]]))


def combine_kernel(mine, one, two, three, sent, own, own_rows):
    state, top, total = merge_messages([m[...] for m in (mine, one, two, three)])
    own[...] = state
    own_rows[...] = in_rows([top, total], 8)
    put_message(sent, state, top, total)


def norm(v, gain):
    mean = jnp.mean(v, axis=-1, keepdims=True)
    centred = v - mean
    spread = jnp.mean(centred * centred, axis=-1, keepdims=True)
    return centred * lax.rsqrt(spread + EPS) * gain


def attention_weights(mine, other, qkv_rows, proj_rows):
    first_core = lax.axis_index("core") == 0
    for lon in range(mine.shape[0]):
        a = mine[lon, :16, :].astype(F32)
        b = other[lon, :16, :].astype(F32)
        tail = jnp.where(first_core, b, a)
        qkv_rows[lon * 24 : lon * 24 + 16, :] = jnp.where(first_core, a, b)
        qkv_rows[lon * 24 + 16 : lon * 24 + 24, :] = tail[:8]
        proj_rows[lon * 8 : lon * 8 + 8, :] = tail[8:]
    return qkv_rows[...].astype(BF16), proj_rows[...].astype(BF16)


def mlp_weights(mine, other):
    width = mine.shape[2]

    def rows(at):
        return jnp.concatenate(
            [w[:, at : at + 16, :].reshape(-1, width) for w in (mine, other)], axis=0
        )

    return rows(16), rows(32)


def attend(q, keys, values, allowed):
    width = q.shape[1]
    per_head = width // HEADS
    scale = per_head ** (-0.5)
    lane_head = lax.broadcasted_iota(jnp.int32, keys.shape, 1) // per_head
    mixed = None
    for h in range(HEADS):
        here = lane_head == h
        k = jnp.where(here, keys, 0.0).astype(BF16)
        v = jnp.where(here, values, 0.0).astype(BF16)
        s = jnp.where(allowed, dot_nt(q, k) * scale, -jnp.inf)
        e = jnp.exp(s - jnp.max(s, axis=1, keepdims=True))
        p = (e / jnp.sum(e, axis=1, keepdims=True)).astype(BF16)
        part = dot_nn(p, v)
        mixed = part if mixed is None else mixed + part
    return mixed.astype(BF16)


def gelu(x):
    return jax.nn.gelu(x, approximate=True)


def after_attention(x, mixed, gain, w_proj, w_up, w_down):
    x1 = x + dot_nn(mixed, w_proj)
    normed = norm(x1, gain).astype(BF16)
    hidden = gelu(dot_nt(normed, w_up)).astype(BF16)
    return x1 + dot_nn(hidden, w_down)


def token_at(shape, dim):
    t = lax.broadcasted_iota(jnp.int32, shape, dim)
    return t // 64, (t & 7) // 4, t


def half_tokens(x, half):
    to = lax.broadcasted_iota(jnp.int32, (64, 128), 0)
    source = lax.broadcasted_iota(jnp.int32, (64, 128), 1)
    pick = (to // 4) * 8 + half * 4 + (to & 3) == source
    return dot_nn(jnp.where(pick, 1.0, 0.0).astype(BF16), x).astype(BF16)


def whole_kernel(own, own_rows, got, state):
    n = own.shape[0]
    got_top, got_total = top_and_total(got[n:, :n])
    rows = own_rows[...]
    state[...], _, _ = merged(
        [own[...], got[:n, :].astype(F32)], [rows[0:1], got_top], [rows[1:2], got_total]
    )


def block0_kernel(start, gains, mine, other, state, far, near, qkv_rows, proj_rows):
    n, width = start.shape
    x = start[...]
    w_qkv, w_proj = attention_weights(mine, other, qkv_rows, proj_rows)
    w_up, w_down = mlp_weights(mine, other)
    a = norm(x, gains[0:1, :]).astype(BF16)
    qkv = dot_nt(a, w_qkv).astype(BF16).astype(F32)
    allowed = token_at((n, n), 0)[0] == token_at((n, n), 1)[0]
    mixed = attend(
        qkv[:, :width].astype(BF16), qkv[:, width : 2 * width], qkv[:, 2 * width :], allowed
    )
    x = after_attention(x, mixed, gains[1:2, :], w_proj, w_up, w_down)
    state[...] = x
    short = x.astype(BF16)
    odd = lax.axis_index("zl") & 1
    near[...] = half_tokens(short, 1 - odd)
    far[...] = half_tokens(short, odd)


def sides_kernel(from_far, from_near, gains, out):
    odd = (lax.axis_index("zl") & 1) == 1
    near, far = from_near[...].astype(F32), from_far[...].astype(F32)
    sides = jnp.concatenate([jnp.where(odd, near, far), jnp.where(odd, far, near)], axis=0)
    out[...] = norm(sides, gains[2:3, :]).astype(BF16)


def block1_kernel(state, sides, gains, mine, other, out, qkv_rows, proj_rows):
    n, width = state.shape
    x = state[...]
    w_qkv, w_proj = attention_weights(mine, other, qkv_rows, proj_rows)
    w_up, w_down = mlp_weights(mine, other)
    a = norm(x, gains[2:3, :]).astype(BF16)
    qkv = dot_nt(a, w_qkv).astype(BF16).astype(F32)
    side_kv = dot_nt(sides[...], w_qkv[width:, :]).astype(BF16).astype(F32)
    keys = jnp.concatenate([qkv[:, width : 2 * width], side_kv[:, :width]], axis=0)
    values = jnp.concatenate([qkv[:, 2 * width :], side_kv[:, width:]], axis=0)
    q_block, q_half, _ = token_at((n, 2 * n), 0)
    k_block, k_half, k_at = token_at((n, 2 * n), 1)
    side = k_at - n
    k_block = jnp.where(k_at < n, k_block, (side & 63) // 32)
    k_half = jnp.where(k_at < n, k_half, side // 64)
    allowed = (q_block == k_block) & (q_half == k_half)
    mixed = attend(qkv[:, :width].astype(BF16), keys, values, allowed)
    x = after_attention(x, mixed, gains[3:4, :], w_proj, w_up, w_down)
    final = norm(x, gains[4:5, :]).astype(BF16)
    for j in range(out.shape[0]):
        out[j] = final


def decode_kernel(tokens, weight, out):
    cores, chips, own, width = tokens.shape
    for c in range(2):
        w = weight[c]
        for y in range(chips):
            for core in range(cores):
                at = (y * cores + core) * own
                out[c, at : at + own, :] = dot_nn(tokens[core, y], w).astype(BF16)


def spread_kernel(count, times, *refs):
    parts, outs = refs[:count], refs[-len(times) :]
    height = outs[0].shape[-2]
    at = 0
    for part in parts:
        n = part.shape[0]
        for layer, (out, repeat) in enumerate(zip(outs, times)):
            rows = part[:, layer * height : (layer + 1) * height, :]
            for k in range(repeat):
                out[k, at : at + n] = rows
        at += n


def spread(parts, times, after=(), flops=0):
    pieces, height, width = parts[0].shape
    total = sum(p.shape[0] for p in parts)
    vmem = pl.BlockSpec(memory_space=pltpu.VMEM)
    return pl.pallas_call(
        functools.partial(spread_kernel, len(parts), times),
        out_shape=[
            jax.ShapeDtypeStruct((n, total, height // len(times), width), BF16) for n in times
        ],
        in_specs=[vmem] * (len(parts) + len(after)),
        out_specs=[vmem] * len(times),
        compiler_params=pltpu.CompilerParams(vmem_limit_bytes=16 * 2**20),
        cost_estimate=pl.CostEstimate(
            flops=flops, bytes_accessed=2 * (1 + sum(times)) * total * height * width, transcendentals=0
        ),
    )(*parts, *after)


def on_core(kernel, outs, scratch=(), flops=0, moved=0, far=()):
    vmem, anywhere = pl.BlockSpec(memory_space=pltpu.VMEM), pl.BlockSpec(memory_space=pl.ANY)

    def call(*operands):
        return pl.pallas_call(
            kernel,
            out_shape=outs,
            in_specs=[anywhere] * len(far) + [vmem] * len(operands),
            out_specs=jax.tree.map(lambda _: vmem, outs),
            scratch_shapes=list(scratch),
            compiler_params=pltpu.CompilerParams(vmem_limit_bytes=40 * 2**20),
            cost_estimate=pl.CostEstimate(flops=flops, bytes_accessed=moved, transcendentals=0),
        )(*far, *operands)

    return call


def shifted(value, axes, size, steps):
    return lax.ppermute(value, axes, [(i, (i + steps) % size) for i in range(size)])


def swaps():
    def at(zh, x, zl):
        return (zh * 4 + x) * 8 + zl

    near, far = [], []
    for zh in range(2):
        for x in range(4):
            near += [(at(zh, x, zl), at(zh, x, zl ^ 1)) for zl in range(8)]
            far += [(at(zh, x, zl), at(zh, x, zl + 1)) for zl in (1, 3, 5)]
            far += [(at(zh, x, zl), at(zh, x, zl - 1)) for zl in (2, 4, 6)]
            far.append((at(zh, x, 7), at(1 - zh, (x + 1) % 4, 0)))
            far.append((at(zh, x, 0), at(1 - zh, (x + 3) % 4, 7)))
    return near, far


def weight_pieces(qkv, proj, up, down):
    core = lax.axis_index("core")
    qkv, up = jnp.swapaxes(qkv, 1, 2), jnp.swapaxes(up, 1, 2)
    attn = jnp.concatenate([qkv, proj], axis=1)
    lanes = [lax.dynamic_slice_in_dim(a, core * 16, 16, 1) for a in (attn, up, down)]
    piece = jnp.concatenate(lanes, axis=1)
    return piece.reshape(1, -1, piece.shape[2])


def body(
    patches,
    embed_weight,
    channel_embed,
    agg_query,
    norm_gains,
    qkv_weight,
    proj_weight,
    up_weight,
    down_weight,
    decode_weight,
):
    chans, rows, cols, width_p = patches.shape
    width = embed_weight.shape[2]
    tokens = rows * cols
    parts = lax.axis_size("y") * lax.axis_size("core")
    own = tokens // parts

    piece = weight_pieces(qkv_weight, proj_weight, up_weight, down_weight)
    (near,) = spread([piece], (8,))
    near = lax.all_to_all(near.reshape(8, -1, width), "zl", 0, 0, tiled=True)

    table = jnp.concatenate(
        [
            embed_weight.reshape(-1, width).astype(F32),
            channel_embed.astype(F32),
            agg_query.reshape(1, width),
            jnp.zeros((8 - chans - 1, width), F32),
        ],
        axis=0,
    )
    message = jax.ShapeDtypeStruct((own + EXTRA, width), BF16)
    messages = jax.ShapeDtypeStruct((4, own + EXTRA, width), BF16)
    stay, leave = on_core(
        embed_kernel,
        (messages, messages),
        [
            pltpu.VMEM((8, tokens), F32),
            pltpu.VMEM((EXTRA, tokens), F32),
        ],
        flops=2 * chans * tokens * width_p * width,
        moved=2 * 2**20,
    )(table, patches.reshape(chans, tokens, width_p))
    got = shifted(leave, "core", 2, 1)
    paired = on_core(pair_kernel, (message,) * 4, moved=2**20)(stay, got)
    along = [shifted(paired[k], "y", 4, k) for k in (1, 2, 3)]
    sent, average, stats = on_core(
        combine_kernel,
        (
            message,
            jax.ShapeDtypeStruct((own, width), F32),
            jax.ShapeDtypeStruct((8, own), F32),
        ),
        flops=6 * 10**10,
    )(paired[0], *along)
    copies0, near1 = spread([near], (4, 1), after=(paired[0],))
    mine0 = lax.all_to_all(copies0, "x", 0, 0, tiled=True).reshape(32, -1, width)
    (copies1,) = spread([near1[0]], (4,), after=(mine0,), flops=0)
    mine1 = lax.all_to_all(copies1, "x", 0, 0, tiled=True).reshape(32, -1, width)
    partner = shifted(sent, "zh", 2, 1)
    other0 = shifted(mine0, "core", 2, 1)
    start = on_core(
        whole_kernel, jax.ShapeDtypeStruct((own, width), F32), flops=6 * 10**10
    )(average, stats, partner)

    scratch = [pltpu.VMEM((3 * width, width), F32), pltpu.VMEM((width, width), F32)]
    half = jax.ShapeDtypeStruct((own // 2, width), BF16)
    block_flops = 2 * own * width * width * 12
    state, to_far, to_near = on_core(
        block0_kernel,
        (jax.ShapeDtypeStruct((own, width), F32), half, half),
        scratch,
        flops=block_flops,
        moved=4 * 2**20,
    )(start, norm_gains, mine0, other0)
    near_pairs, far_pairs = swaps()
    from_far = lax.ppermute(to_far, ("zh", "x", "zl"), far_pairs)
    from_near = lax.ppermute(to_near, ("zh", "x", "zl"), near_pairs)
    other1 = shifted(mine1, "core", 2, 1)
    sides = on_core(
        sides_kernel, jax.ShapeDtypeStruct((own, width), BF16), flops=6 * 10**10
    )(from_far, from_near, norm_gains)
    final = on_core(
        block1_kernel,
        jax.ShapeDtypeStruct((4, own, width), BF16),
        scratch,
        flops=block_flops,
        moved=4 * 2**20,
    )(state, sides, norm_gains, mine1, other1)
    everyone = lax.all_gather(lax.all_to_all(final, "y", 0, 0, tiled=True), "core")
    decoded = on_core(
        decode_kernel,
        jax.ShapeDtypeStruct((chans, tokens, width_p), BF16),
        flops=2 * chans * tokens * width_p * width,
        moved=2 * 2**20,
    )(everyone, decode_weight)
    return decoded.reshape(chans, rows, cols, width_p)


def solution(mesh):
    fine = Mesh(mesh.devices.reshape(2, 4, 2, 4, 8), ("zh", "y", "core", "x", "zl"))
    chan, lon = ("zh", "y", "core"), ("x", "zl")
    placed = (
        P(chan, None, lon, None),
        P(chan, None, None),
        P(chan, None),
        P(),
        P(),
        P(None, None, lon),
        P(None, lon, None),
        P(None, None, lon),
        P(None, lon, None),
        P(chan, None, None),
    )
    return jax.shard_map(
        body, mesh=fine, in_specs=placed, out_specs=P(chan, None, lon, None), check_vma=False
    )
```
